32 devices in a mesh: dp: 4 (over y, x), expert: 8 (over z, core).
Axes of the slice: x: 2, y: 2, z: 4, core: 2. Of those that a mesh axis runs over, the one named last changes fastest.
Arguments:
- tokens: bfloat16 [4096, 3584], P(('dp', 'expert')), may hold values from -6 to 6
- cotangent: bfloat16 [4096, 3584], P(('dp', 'expert')), may hold values from -6 to 6
- route_weight: float32 [4096, 8], P(('dp', 'expert')), may hold values from 0.05 to 0.5
- expert_ids: int32 [4096, 8], P(('dp', 'expert')), may hold values from 0 to 255, as said below
- live_tokens: int32 [32], P(('dp', 'expert')), may hold values from 1 to 128, 3072 in all
- replica_plan: int32 [32, 1], P(('dp', 'expert')), may hold values 0 or 1
- w_gate: bfloat16 [3584, 2048], P('dp', 'expert'), may hold values from -0.09375 to 0.09375
- w_up: bfloat16 [3584, 2048], P('dp', 'expert'), may hold values from -0.09375 to 0.09375
- w_down: bfloat16 [2048, 3584], P('expert', 'dp'), may hold values from -0.125 to 0.125
- scale_gate: float32 [28, 16], P(None, 'expert'), may hold values from 0.5 to 2
- scale_up: float32 [28, 16], P(None, 'expert'), may hold values from 0.5 to 2
- scale_down: float32 [16, 28], P('expert'), may hold values from 0.5 to 2
Outputs:
- d_tokens: bfloat16 [4096, 3584], P(('dp', 'expert'))
- grad_gate: bfloat16 [3584, 2048], P('dp', 'expert')
- grad_up: bfloat16 [3584, 2048], P('dp', 'expert')
- grad_down: bfloat16 [2048, 3584], P('expert', 'dp')
The draws below stay inside these ranges and needn't reach their ends.
Inputs may be any that keep to these rules, and one draw needn't show every extreme that they name: `expert_ids`: the 8 ids of one token are distinct.
All inputs are finite; a program needn't handle non-finite values. No bound on the sum of `live_tokens` or of `replica_plan` on one device may be relied on, other than what follows from the above.
Results may differ from the reference program's by a relative error of at most 0.012.
Values may be sent and summed in bfloat16 or wider, within the bound.
No kernel may reach another device: no remote copies, remote signals or barrier semaphores. Data moves between devices by JAX's collectives and lax.ppermute only.
A program may use at most 64 MiB of HBM per device.

```python
import math
import jax
import jax.numpy as jnp
import numpy as np
from jax import lax

D = 3584
EXP_HID = 2048
EXPERTS_ALL = 256
TOPK = 8
HSH = 8
BLOCK = 128
TOK_DEV = 128
CAP = 4
HID = 256
EXPERTS = 1
TOKENS = 4096
N_DP = 4
N_EXPERT = 8


def draw_expert_ids(key, part):
    key_select, key_busiest, key_offset = jax.random.split(key, 3)
    outside_count = EXPERTS_ALL - EXPERTS
    selector = jax.random.randint(key_select, (TOKENS,), 0, TOK_DEV // CAP)
    busiest = jax.random.randint(key_busiest, (), 0, EXPERTS)
    offset_draw = jax.random.randint(key_offset, (TOKENS,), 0, outside_count)
    outside = EXPERTS + (offset_draw[:, None] + jnp.arange(TOPK, dtype=jnp.int32)[None, :]) % outside_count
    leading = jnp.where(selector < EXPERTS, selector, jnp.where(selector < 2 * EXPERTS, busiest, outside[:, TOPK - 1]))
    return jnp.concatenate([leading[:, None], outside[:, :TOPK - 1]], axis=1).astype(jnp.int32)


def touch_ends(array, key, least, high):
    longest = array.shape.index(max(array.shape))
    spots = []
    for shift in (0, 1):
        where = [jax.random.randint(jax.random.fold_in(key, axis), (), 0, length) for axis, length in enumerate(array.shape)]
        where[longest] = (where[longest] + shift) % array.shape[longest]
        spots.append(tuple(where))
    return array.at[spots[0]].set(least).at[spots[1]].set(high)


def levels(own_key, shape, pieces, least, largest):
    factor_of, own = 1.0, jax.random.fold_in(own_key, 6)
    for dim, shards_of in pieces:
        heights = jnp.exp(jax.random.uniform(jax.random.fold_in(own, dim), (shards_of,), jnp.float32, least / len(pieces), largest / len(pieces)))
        factor_of = factor_of * jnp.repeat(heights, shape[dim] // shards_of).reshape([-1 if axis == dim else 1 for axis in range(len(shape))])
    return factor_of


def profile(amount, total, bound, lean):
    portions = [(1 << 20) // math.isqrt(standing ** lean) + 1 for standing in range(2, amount + 1)]
    rest, given = total - bound - (amount - 1), [1] * (amount - 1)
    while rest > 0:
        movable = [i for i in range(amount - 1) if given[i] < bound]
        mass, budget = sum([portions[i] for i in movable]), rest
        for i in movable:
            more = min(bound - given[i], max(1, budget * portions[i] // mass), rest)
            given[i] = given[i] + more
            rest = rest - more
    return np.array([bound] + given)


def uneven_parts(stream_key, number_of, total, reach, skew):
    if number_of == 2:
        one = jax.random.randint(stream_key, (), max(1, total - reach), min(reach, total - 1) + 1)
        return jnp.stack([one, total - one])
    sizes = jnp.asarray(profile(number_of, total, reach, skew), jnp.int32)
    pairs = (number_of - 1) // 2
    donor, sink = sizes[1:1 + 2 * pairs:2], sizes[2:2 + 2 * pairs:2]
    room = jnp.minimum(donor - 1, reach - sink)
    shifted = jax.random.randint(jax.random.fold_in(stream_key, 1), (pairs,), 0, 1 << 20) % (room + 1)
    sizes = sizes.at[1:1 + 2 * pairs:2].set(donor - shifted).at[2:2 + 2 * pairs:2].set(sink + shifted)
    return sizes[jax.random.permutation(jax.random.fold_in(stream_key, 2), number_of)]


def scatter_about(own_key, shape, scale, limit, cuts=(), kind=jnp.bfloat16):
    values = jax.random.normal(own_key, shape, jnp.float32) * scale
    if len(cuts) > 0:
        values = levels(own_key, shape, cuts, -0.22, 0.18) * values
    return jnp.clip(values, min=-limit, max=limit).astype(kind)


def setup_inputs(seed: int = 0) -> dict:
    key_list = jax.random.split(jax.random.key(seed), 13)
    tokens = scatter_about(key_list[0], (TOKENS, D), 1.0, 6.0, ((0, 32),))
    cotangent = scatter_about(key_list[1], (TOKENS, D), 1.0, 6.0, ((0, 32),))
    route_weight = jnp.clip(jnp.exp(math.log(0.5) - 2.3025851 * jax.random.uniform(key_list[2], (TOKENS, TOPK), jnp.float32) ** levels(key_list[2], (TOKENS, TOPK), ((0, 32),), -0.2, 0.2)), 0.05, 0.5)
    expert_ids = draw_expert_ids(jax.random.fold_in(key_list[12], 71), 0)
    live_tokens = uneven_parts(key_list[4], N_DP * N_EXPERT, N_DP * N_EXPERT * TOK_DEV * 3 // 4, TOK_DEV, 0).astype(jnp.int32)
    replica_plan = touch_ends((jax.random.randint(key_list[5], (N_DP * N_EXPERT, EXPERTS), 0, 2) < 1).astype(jnp.int32), jax.random.fold_in(key_list[5], 1), 0, 1)
    w_gate = scatter_about(key_list[6], (D, N_EXPERT * HID), D ** -0.5, 0.09375, ((0, 4), (1, 8)))
    w_up = scatter_about(key_list[7], (D, N_EXPERT * HID), D ** -0.5, 0.09375, ((0, 4), (1, 8)))
    w_down = scatter_about(key_list[8], (N_EXPERT * HID, D), EXP_HID ** -0.5, 0.125, ((0, 8), (1, 4)))
    scale_gate = jnp.clip(jnp.exp(math.log(2.0) - 1.3862944 * jax.random.uniform(key_list[9], (D // BLOCK, N_EXPERT * HID // BLOCK), jnp.float32) ** levels(key_list[9], (D // BLOCK, N_EXPERT * HID // BLOCK), ((1, 8),), -0.2, 0.2)), 0.5, 2.0)
    scale_up = jnp.clip(jnp.exp(math.log(2.0) - 1.3862944 * jax.random.uniform(key_list[10], (D // BLOCK, N_EXPERT * HID // BLOCK), jnp.float32) ** levels(key_list[10], (D // BLOCK, N_EXPERT * HID // BLOCK), ((1, 8),), -0.2, 0.2)), 0.5, 2.0)
    scale_down = jnp.clip(jnp.exp(math.log(2.0) - 1.3862944 * jax.random.uniform(key_list[11], (N_EXPERT * HID // BLOCK, D // BLOCK), jnp.float32) ** levels(key_list[11], (N_EXPERT * HID // BLOCK, D // BLOCK), ((0, 8),), -0.2, 0.2)), 0.5, 2.0)
    return dict(tokens=tokens, cotangent=cotangent, route_weight=route_weight, expert_ids=expert_ids, live_tokens=live_tokens, replica_plan=replica_plan, w_gate=w_gate, w_up=w_up, w_down=w_down, scale_gate=scale_gate, scale_up=scale_up, scale_down=scale_down)


def dequantize(values, scale):
    block_rows = values.shape[0] // scale.shape[0]
    block_cols = values.shape[1] // scale.shape[1]
    spread = jnp.repeat(jnp.repeat(scale, block_rows, axis=0), block_cols, axis=1)
    return (values.astype(jnp.float32) * spread).astype(jnp.bfloat16)


def route_rows(tokens, cotangent, route_weight, expert_ids, live_count, plan, experts, capacity):
    count = tokens.shape[0]
    token_index = jnp.arange(count, dtype=jnp.int32)
    expert_index = jnp.arange(experts, dtype=jnp.int32)
    matches = expert_ids[:, None, :] == expert_index[None, :, None]
    routed = jnp.any(matches, axis=2) & (token_index < live_count)[:, None]
    to_replica = ((token_index % 2) == 1)[:, None] & (plan[None, :] == 1)
    in_lists = jnp.stack([routed & (~to_replica), routed & to_replica], axis=2).astype(jnp.int32)
    position = jnp.cumsum(in_lists, axis=0) - 1
    capacity_index = jnp.arange(capacity, dtype=jnp.int32)
    selected = ((in_lists[..., None] == 1) & (position[..., None] == capacity_index)).astype(jnp.float32)
    weight_sum = jnp.sum(jnp.where(matches, route_weight[:, None, :], jnp.float32(0.0)), axis=2)
    row_weight = jnp.sum(selected * weight_sum[:, :, None, None], axis=0)
    flat = selected.reshape(count, -1)
    picker = flat.T.astype(jnp.bfloat16)
    token_rows = jnp.dot(picker, tokens, preferred_element_type=jnp.float32).astype(jnp.bfloat16)
    cot_picked = jnp.dot(picker, cotangent, preferred_element_type=jnp.float32)
    cot_rows = (row_weight.reshape(-1, 1) * cot_picked).astype(jnp.bfloat16)
    shape = (experts, 2, capacity, tokens.shape[1])
    return flat, token_rows.reshape(shape), cot_rows.reshape(shape)


def expert_terms(token_rows, cot_rows, gate_w, up_w, down_w, shards):
    gate_pre = jnp.dot(token_rows, gate_w, preferred_element_type=jnp.float32)
    up_pre = jnp.dot(token_rows, up_w, preferred_element_type=jnp.float32)
    gate_sig = jax.nn.sigmoid(gate_pre)
    swish = gate_pre * gate_sig
    d_hidden = jnp.dot(cot_rows, down_w.T, preferred_element_type=jnp.float32)
    hidden = (swish * up_pre).astype(jnp.bfloat16)
    d_up = (d_hidden * swish).astype(jnp.bfloat16)
    d_gate = (d_hidden * up_pre * gate_sig * (1.0 + gate_pre * (1.0 - gate_sig))).astype(jnp.bfloat16)
    grad_g = jnp.dot(token_rows.T, d_gate, preferred_element_type=jnp.float32).astype(jnp.bfloat16)
    grad_u = jnp.dot(token_rows.T, d_up, preferred_element_type=jnp.float32).astype(jnp.bfloat16)
    grad_d = jnp.dot(hidden.T, cot_rows, preferred_element_type=jnp.float32).astype(jnp.bfloat16)
    rows = token_rows.shape[0]
    width = token_rows.shape[1]
    gate_parts = jnp.einsum("rkh,dkh->krd", d_gate.astype(jnp.float32).reshape(rows, shards, -1),
                            gate_w.astype(jnp.float32).reshape(width, shards, -1), precision=lax.Precision.HIGHEST)
    up_parts = jnp.einsum("rkh,dkh->krd", d_up.astype(jnp.float32).reshape(rows, shards, -1),
                          up_w.astype(jnp.float32).reshape(width, shards, -1), precision=lax.Precision.HIGHEST)
    parts = (gate_parts + up_parts).astype(jnp.bfloat16).astype(jnp.float32)
    return grad_g, grad_u, grad_d, jnp.sum(parts, axis=0)


def reference(tokens, cotangent, route_weight, expert_ids, live_tokens, replica_plan, w_gate, w_up, w_down,
              scale_gate, scale_up, scale_down):
    devices = N_DP * N_EXPERT
    width = tokens.shape[1]

    def per_device(tok_block, cot_block, weight_block, id_block, live_count, plan_row):
        return route_rows(tok_block, cot_block, weight_block, id_block, live_count, plan_row, EXPERTS, CAP)

    flat, token_rows, cot_rows = jax.vmap(per_device)(
        tokens.reshape(devices, TOK_DEV, width), cotangent.reshape(devices, TOK_DEV, width),
        route_weight.reshape(devices, TOK_DEV, TOPK), expert_ids.reshape(devices, TOK_DEV, TOPK), live_tokens,
        replica_plan)
    token_rows = token_rows.reshape(N_DP, N_EXPERT, EXPERTS, 2, CAP, width)
    cot_rows = cot_rows.reshape(N_DP, N_EXPERT, EXPERTS, 2, CAP, width)
    gate_all = dequantize(w_gate, scale_gate)
    up_all = dequantize(w_up, scale_up)
    down_all = dequantize(w_down, scale_down)
    gate_list, up_list, down_list, row_list = [], [], [], []
    for expert in range(EXPERTS):
        start = expert * EXP_HID
        gate_w = gate_all[:, start:start + EXP_HID]
        up_w = up_all[:, start:start + EXP_HID]
        down_w = down_all[start:start + EXP_HID, :]

        def group(pair):
            rows_x, rows_c = pair
            leading = expert_terms(rows_x[:, 0].reshape(-1, width), rows_c[:, 0].reshape(-1, width),
                                   gate_w, up_w, down_w, HSH)
            trailing = expert_terms(rows_x[:, 1].reshape(-1, width), rows_c[:, 1].reshape(-1, width),
                                    gate_w, up_w, down_w, HSH)
            sum_gate = (leading[0].astype(jnp.float32) + trailing[0].astype(jnp.float32)).astype(jnp.bfloat16)
            sum_up = (leading[1].astype(jnp.float32) + trailing[1].astype(jnp.float32)).astype(jnp.bfloat16)
            sum_down = (leading[2].astype(jnp.float32) + trailing[2].astype(jnp.float32)).astype(jnp.bfloat16)
            dx_rows = jnp.stack([leading[3].reshape(N_EXPERT, CAP, width),
                                 trailing[3].reshape(N_EXPERT, CAP, width)], axis=1)
            return sum_gate, sum_up, sum_down, dx_rows

        result = lax.map(group, (token_rows[:, :, expert], cot_rows[:, :, expert]))
        gate_list.append(jnp.sum(result[0].astype(jnp.float32), axis=0).astype(jnp.bfloat16))
        up_list.append(jnp.sum(result[1].astype(jnp.float32), axis=0).astype(jnp.bfloat16))
        down_list.append(jnp.sum(result[2].astype(jnp.float32), axis=0).astype(jnp.bfloat16))
        row_list.append(result[3])
    dx_rows = jnp.stack(row_list, axis=2).reshape(devices, -1, width)

    def gather_back(selection, rows):
        return jnp.dot(selection, rows, precision=lax.Precision.HIGHEST)

    d_tokens = jax.vmap(gather_back)(flat, dx_rows).astype(jnp.bfloat16).reshape(TOKENS, width)
    grad_gate = jnp.concatenate(gate_list, axis=1)
    grad_up = jnp.concatenate(up_list, axis=1)
    grad_down = jnp.concatenate(down_list, axis=0)
    return (d_tokens, grad_gate, grad_up, grad_down)
```

```python
import functools
import math

import jax
import jax.numpy as jnp
from jax import lax
from jax.experimental import pallas as pl
from jax.experimental.pallas import tpu as pltpu
from jax.sharding import PartitionSpec as P

HSH = 8
CAP = 4
ROWS = 2 * CAP
BLOCK = 128
CHIPS = HSH // 2
BF16 = jnp.bfloat16
F32 = jnp.float32
VMEM_BYTES = 48 * 1024 * 1024

NN = (((1,), (0,)), ((), ()))
NT = (((1,), (1,)), ((), ()))
TN = (((0,), (0,)), ((), ()))


def mm(a, b, dims):
    return lax.dot_general(a, b, dims, preferred_element_type=F32)


def call(kernel, outs, scalars, arrays, scratch=(), flops=0, name=None):
    moved = sum(math.prod(x.shape) * x.dtype.itemsize for x in (*arrays, *outs))
    return pl.pallas_call(
        kernel,
        out_shape=outs,
        in_specs=[pl.BlockSpec(memory_space=pltpu.SMEM)] * len(scalars)
        + [pl.BlockSpec(memory_space=pltpu.VMEM)] * len(arrays),
        out_specs=[pl.BlockSpec(memory_space=pltpu.VMEM)] * len(outs),
        scratch_shapes=list(scratch),
        compiler_params=pltpu.CompilerParams(vmem_limit_bytes=VMEM_BYTES),
        cost_estimate=pl.CostEstimate(flops=flops, bytes_accessed=moved, transcendentals=0),
        name=name,
    )(*scalars, *arrays)


def shape(dims, dtype=BF16):
    return jax.ShapeDtypeStruct(dims, dtype)


def swap(x, axis, k):
    return lax.ppermute(x, axis, [(i, i ^ k) for i in range(lax.axis_size(axis))])


def rows_of(value, first, count=ROWS):
    return value[first : first + count]


def route_kernel(groups, experts, live, plan, me, ids, weight, tokens, cots, *rest):
    outs, picks, slices = rest[:groups], rest[groups], rest[groups + 1]
    count, width = tokens.shape
    depth = width // groups
    lists = experts * ROWS
    slot = lax.broadcasted_iota(jnp.int32, (count, 1), 0)
    lane = lax.broadcasted_iota(jnp.int32, (count, lists), 1)
    alive = slot < live[0]
    odd = slot % 2 == 1
    listed = jnp.zeros((count, lists), F32)
    weights = jnp.zeros((count, lists), F32)
    for e in range(experts):
        match = ids[...] == e
        routed = (jnp.sum(jnp.where(match, 1.0, 0.0), axis=1, keepdims=True) > 0.0) & alive
        total = jnp.sum(jnp.where(match, weight[...], 0.0), axis=1, keepdims=True)
        second = odd & (plan[0, e] == 1)
        in_first = jnp.where(routed & ~second, 1.0, 0.0)
        in_second = jnp.where(routed & second, 1.0, 0.0)
        is_first = (lane >= e * ROWS) & (lane < e * ROWS + CAP)
        is_second = (lane >= e * ROWS + CAP) & (lane < (e + 1) * ROWS)
        listed = jnp.where(is_first, in_first, jnp.where(is_second, in_second, listed))
        weights = jnp.where(is_first | is_second, total, weights)
    before = lax.broadcasted_iota(jnp.int32, (count, count), 1)
    here = lax.broadcasted_iota(jnp.int32, (count, count), 0)
    upto = jnp.where(before <= here, 1.0, 0.0).astype(BF16)
    place = mm(upto, listed.astype(BF16), NN)
    wanted = (lane % CAP + 1).astype(F32)
    picked = jnp.where((listed > 0.0) & (place == wanted), 1.0, 0.0)
    row_weight = jnp.sum(picked * weights, axis=0, keepdims=True)
    square = (lists, lists)
    eye = lax.broadcasted_iota(jnp.int32, square, 0) == lax.broadcasted_iota(jnp.int32, square, 1)
    column = jnp.sum(jnp.where(eye, row_weight, 0.0), axis=1, keepdims=True)
    picked = picked.astype(BF16)
    for e in range(experts):
        picks[e] = picked[:, e * ROWS : (e + 1) * ROWS]
    for s in range(groups):
        cut = slice(s * depth, (s + 1) * depth)
        token_rows = mm(picked, tokens[:, cut], TN)
        cot_rows = mm(picked, cots[:, cut], TN) * column
        parts = []
        for e in range(experts):
            parts += [rows_of(token_rows, e * ROWS), rows_of(cot_rows, e * ROWS)]
        slices[s] = jnp.concatenate(parts, axis=0).astype(BF16)
    for k in range(groups):
        outs[k][...] = slices[me[0] ^ k]


def weights_kernel(first, scale_gate, scale_up, scale_down, gate, up, down, gate_up, down_out):
    depth, hid = gate.shape
    step = math.gcd(depth, BLOCK)
    for i in range(depth // step):
        block = (first[0] + i * step) // BLOCK
        for h in range(hid // BLOCK):
            at = (slice(i * step, (i + 1) * step), slice(h * BLOCK, (h + 1) * BLOCK))
            to = slice(hid + h * BLOCK, hid + (h + 1) * BLOCK)
            gate_up[at] = (gate[at].astype(F32) * scale_gate[block, h]).astype(BF16)
            gate_up[at[0], to] = (up[at].astype(F32) * scale_up[block, h]).astype(BF16)
    lane = lax.broadcasted_iota(jnp.int32, (1, depth), 1)
    start = first[0] // BLOCK
    last = scale_down.shape[1] - 1
    for h in range(hid // BLOCK):
        spread = jnp.zeros((1, depth), F32) + scale_down[h, start]
        for j in range(1, depth // BLOCK + 2):
            block = jnp.minimum(start + j, last)
            spread = jnp.where(lane >= (start + j) * BLOCK - first[0], scale_down[h, block], spread)
        at = slice(h * BLOCK, (h + 1) * BLOCK)
        down_out[at, :] = (down[at, :].astype(F32) * spread).astype(BF16)


def token_part(chunks):
    return jnp.concatenate([c[: c.shape[0] // 2, :] for c in chunks], axis=0)


def cot_part(chunks):
    return jnp.concatenate([c[c.shape[0] // 2 :, :] for c in chunks], axis=0)


def partial_kernel(groups, chips, *refs):
    chunks, weights, outs = refs[:chips], refs[chips : chips + 4], refs[chips + 4 :]
    tokens, cots = token_part(chunks), cot_part(chunks)
    hid = weights[1].shape[0]
    for half in range(2):
        gate_up, down = weights[2 * half], weights[2 * half + 1]
        for product, at in (
            (mm(tokens, gate_up[...], NN), 0),
            (mm(cots, down[...], NT), 2 * hid),
        ):
            cut = slice(3 * hid * half + at, 3 * hid * half + at + product.shape[1])
            for k in range(groups):
                rows = [rows_of(product, (c * groups + k) * ROWS) for c in range(chips)]
                outs[k][:, cut] = jnp.concatenate(rows, axis=0).astype(outs[k].dtype)


def act_kernel(groups, *refs):
    parts, out = refs[:groups], refs[groups]
    hid = out.shape[1] // 6
    for half in range(2):
        values = []
        for i in range(3):
            cut = slice((3 * half + i) * hid, (3 * half + i + 1) * hid)
            total = parts[0][:, cut]
            for part in parts[1:]:
                total = total + part[:, cut].astype(F32)
            values.append(total)
        a, b, dh = values
        sig = jax.nn.sigmoid(a)
        swish = a * sig
        results = (dh * b * sig * (1.0 + a * (1.0 - sig)), dh * swish, swish * b)
        for i, result in enumerate(results):
            cut = slice((3 * half + i) * hid, (3 * half + i + 1) * hid)
            out[:, cut] = result.astype(BF16)


def dx_kernel(groups, chips, *refs):
    acts, (own, other), outs = refs[:groups], refs[groups : groups + 2], refs[groups + 2 :]
    hid = own.shape[1] // 2
    act = jnp.concatenate([a[...] for a in acts], axis=0)
    outs[chips][...] = act[:, 3 * hid :]
    dx = mm(act[:, : 2 * hid], own[...], NT) + mm(act[:, 3 * hid : 5 * hid], other[...], NT)
    for c in range(chips):
        rows = [rows_of(dx, (k * chips + c) * ROWS) for k in range(groups)]
        outs[c][...] = jnp.concatenate(rows, axis=0).astype(outs[c].dtype)


def collect_kernel(groups, chips, *refs):
    parts, outs = refs[:chips], refs[chips:]
    sums = []
    for first in range(0, chips, CHIPS):
        total = parts[first][...].astype(F32)
        for part in parts[first + 1 : first + CHIPS]:
            total = total + part[...].astype(F32)
        sums.append(total)
    for k in range(groups):
        rows = [rows_of(total, k * ROWS) for total in sums]
        outs[k][...] = jnp.concatenate(rows, axis=0).astype(BF16)


def place_kernel(groups, experts, me, home, *refs):
    parts, picks, out, slices = refs[:groups], refs[groups], refs[groups + 1], refs[groups + 2]
    depth = parts[0].shape[1]
    for k in range(groups):
        slices[me[0] ^ k] = parts[k][...].astype(F32)
    for s in range(groups):
        total = jnp.zeros((out.shape[0], depth), F32)
        for x in range(experts):
            rows = slices[s, x * ROWS : (x + 1) * ROWS, :].astype(BF16)
            total = total + mm(picks[home[0] ^ x], rows, NN)
        out[:, s * depth : (s + 1) * depth] = total.astype(BF16)


def regroup(act, groups, chips):
    wide = act.astype(F32)
    rows = [rows_of(wide, (k * chips + c) * ROWS) for c in range(chips) for k in range(groups)]
    return jnp.concatenate(rows, axis=0).astype(BF16)


def grads_kernel(groups, chips, *refs):
    own, other = refs[:chips], refs[chips : 2 * chips]
    acts, act_other = refs[2 * chips : 2 * chips + groups], refs[2 * chips + groups]
    grad_gate, grad_up, grad_down = refs[2 * chips + groups + 1 :]
    hid = grad_gate.shape[1]
    act = jnp.concatenate([a[:, : 3 * hid] for a in acts], axis=0)
    tokens = jnp.concatenate([token_part(own), token_part(other)], axis=0)
    cots = jnp.concatenate([cot_part(own), cot_part(other)], axis=0)
    both = jnp.concatenate(
        [regroup(act, groups, chips), regroup(act_other[...], groups, chips)], axis=0
    )
    grad_gate[...] = mm(tokens, both[:, :hid], TN).astype(BF16)
    grad_up[...] = mm(tokens, both[:, hid : 2 * hid], TN).astype(BF16)
    grad_down[...] = mm(both[:, 2 * hid :], cots, TN).astype(BF16)


def chunk_of(parts, experts, slot):
    blocks = [p.reshape(experts, 2, ROWS, p.shape[1]) for p in parts]
    if experts == 1:
        blocks = [b[0] for b in blocks]
    else:
        blocks = [lax.dynamic_index_in_dim(b, slot, 0, keepdims=False) for b in blocks]
    return jnp.concatenate([b[0] for b in blocks] + [b[1] for b in blocks], axis=0)


def on_device(
    tokens,
    cotangent,
    route_weight,
    expert_ids,
    live_tokens,
    replica_plan,
    w_gate,
    w_up,
    w_down,
    scale_gate,
    scale_up,
    scale_down,
):
    members, groups = lax.axis_size("expert"), lax.axis_size("dp")
    experts, chips = members // HSH, members // 2
    count, width = tokens.shape
    depth, hid = w_gate.shape
    group, member = lax.axis_index("dp"), lax.axis_index("expert")
    me = jnp.reshape(group, (1,))
    home = jnp.reshape(member // HSH, (1,))
    rows = groups * chips * ROWS

    *sent, picks = call(
        functools.partial(route_kernel, groups, experts),
        [shape((2 * ROWS * experts, depth))] * groups + [shape((experts, count, ROWS))],
        (live_tokens, replica_plan, me),
        (expert_ids, route_weight, tokens, cotangent),
        scratch=[pltpu.VMEM((groups, 2 * ROWS * experts, depth), BF16)],
        flops=4 * count * experts * ROWS * width,
        name="route",
    )
    parts = [sent[0]] + [swap(sent[k], "dp", k) for k in range(1, groups)]

    gate_up, down = call(
        weights_kernel,
        [shape((depth, 2 * hid)), shape((hid, depth))],
        (me * depth, scale_gate, scale_up, scale_down),
        (w_gate, w_up, w_down),
        flops=6 * depth * hid,
        name="weights",
    )
    other_gate_up, other_down = swap(gate_up, "expert", 1), swap(down, "expert", 1)

    chunks = [chunk_of(parts, experts, member // HSH)]
    for c in range(1, chips):
        out = chunks[0] if experts == 1 else chunk_of(parts, experts, (member ^ (2 * c)) // HSH)
        chunks.append(swap(out, "expert", 2 * c))

    partial = call(
        functools.partial(partial_kernel, groups, chips),
        [shape((chips * ROWS, 6 * hid), F32 if k == 0 else BF16) for k in range(groups)],
        (),
        (*chunks, gate_up, down, other_gate_up, other_down),
        flops=12 * rows * depth * hid,
        name="partial",
    )
    summands = [partial[0]] + [swap(partial[k], "dp", k) for k in range(1, groups)]
    (act,) = call(
        functools.partial(act_kernel, groups),
        [shape((chips * ROWS, 6 * hid))],
        (),
        summands,
        flops=40 * chips * ROWS * hid,
        name="activations",
    )
    acts = [act] + [swap(act, "dp", k) for k in range(1, groups)]
    *dx, act_out = call(
        functools.partial(dx_kernel, groups, chips),
        [shape((groups * ROWS, depth), F32 if c == 0 else BF16) for c in range(chips)]
        + [shape((rows, 3 * hid))],
        (),
        (*acts, gate_up, other_gate_up),
        flops=8 * rows * depth * hid,
        name="dx",
    )
    returned = [dx[0]] + [swap(dx[c], "expert", 2 * c) for c in range(1, chips)]

    other_chunks = [swap(c, "expert", 1) for c in chunks]
    act_other = swap(act_out, "expert", 1)

    home_rows = call(
        functools.partial(collect_kernel, groups, chips),
        [shape((experts * ROWS, depth))] * groups,
        (),
        returned,
        flops=rows * depth,
        name="collect",
    )
    placed = [home_rows[0]] + [swap(home_rows[k], "dp", k) for k in range(1, groups)]

    grad_gate, grad_up, grad_down = call(
        functools.partial(grads_kernel, groups, chips),
        [shape((depth, hid)), shape((depth, hid)), shape((hid, depth))],
        (),
        (*chunks, *other_chunks, *acts, act_other),
        flops=12 * rows * depth * hid,
        name="gradients",
    )
    (d_tokens,) = call(
        functools.partial(place_kernel, groups, experts),
        [shape((count, width))],
        (me, home),
        (*placed, picks),
        scratch=[pltpu.VMEM((groups, experts * ROWS, depth), F32)],
        flops=2 * count * experts * ROWS * width,
        name="place",
    )
    return (d_tokens, grad_gate, grad_up, grad_down)


def solution(mesh):
    return jax.shard_map(
        on_device,
        mesh=mesh,
        in_specs=(
            P(("dp", "expert"), None),
            P(("dp", "expert"), None),
            P(("dp", "expert"), None),
            P(("dp", "expert"), None),
            P(("dp", "expert")),
            P(("dp", "expert"), None),
            P("dp", "expert"),
            P("dp", "expert"),
            P("expert", "dp"),
            P(None, "expert"),
            P(None, "expert"),
            P("expert", None),
        ),
        out_specs=(
            P(("dp", "expert"), None),
            P("dp", "expert"),
            P("dp", "expert"),
            P("expert", "dp"),
        ),
        check_vma=False,
    )
```

```python
import functools
import math

import jax
import jax.numpy as jnp
from jax import lax
from jax.experimental import pallas as pl
from jax.experimental.pallas import tpu as pltpu
from jax.sharding import PartitionSpec as P

HSH = 8
CAP = 4
ROWS = 2 * CAP
BLOCK = 128
CHIPS = HSH // 2
BF16 = jnp.bfloat16
F32 = jnp.float32
VMEM_BYTES = 48 * 1024 * 1024

NN = (((1,), (0,)), ((), ()))
NT = (((1,), (1,)), ((), ()))
TN = (((0,), (0,)), ((), ()))


def mm(a, b, dims):
    return lax.dot_general(a, b, dims, preferred_element_type=F32)


def call(kernel, outs, scalars, arrays, far=(), scratch=(), flops=0, name=None):
    moved = sum(math.prod(x.shape) * x.dtype.itemsize for x in (*arrays, *outs))
    return pl.pallas_call(
        kernel,
        out_shape=outs,
        in_specs=[pl.BlockSpec(memory_space=pltpu.SMEM)] * len(scalars)
        + [pl.BlockSpec(memory_space=pl.ANY)] * len(far)
        + [pl.BlockSpec(memory_space=pltpu.VMEM)] * len(arrays),
        out_specs=[pl.BlockSpec(memory_space=pltpu.VMEM)] * len(outs),
        scratch_shapes=list(scratch),
        compiler_params=pltpu.CompilerParams(vmem_limit_bytes=VMEM_BYTES),
        cost_estimate=pl.CostEstimate(flops=flops, bytes_accessed=moved, transcendentals=0),
        name=name,
    )(*scalars, *far, *arrays)


def shape(dims, dtype=BF16):
    return jax.ShapeDtypeStruct(dims, dtype)


def swap(x, axis, k):
    return lax.ppermute(x, axis, [(i, i ^ k) for i in range(lax.axis_size(axis))])


def rows_of(value, first, count=ROWS):
    return value[first : first + count]


def route_kernel(groups, experts, me, live_in, plan_in, ids_in, weight_in, tokens_in, cots_in, *rest):
    outs, picks, scratch = rest[:groups], rest[groups], rest[groups + 1 :]
    live, plan, ids, weight, tokens, cots, slices, sems = scratch
    sources = (live_in, plan_in, ids_in, weight_in, tokens_in, cots_in)
    targets = (live, plan, ids, weight, tokens, cots)
    copies = [pltpu.make_async_copy(s, t, sems.at[i]) for i, (s, t) in enumerate(zip(sources, targets))]
    for copy in copies:
        copy.start()
    for copy in copies[:4]:
        copy.wait()
    count, width = tokens.shape
    depth = width // groups
    lists = experts * ROWS
    slot = lax.broadcasted_iota(jnp.int32, (1, count), 1)
    line = lax.broadcasted_iota(jnp.int32, (lists, count), 0)
    alive = slot < live[0]
    odd = slot % 2 == 1
    listed = jnp.zeros((lists, count), F32)
    weights = jnp.zeros((lists, count), F32)
    for e in range(experts):
        match = ids[...] == e
        routed = (jnp.sum(jnp.where(match, 1.0, 0.0), axis=0, keepdims=True) > 0.0) & alive
        total = jnp.sum(jnp.where(match, weight[...], 0.0), axis=0, keepdims=True)
        second = odd & (plan[0, e] == 1)
        in_first = jnp.where(routed & ~second, 1.0, 0.0)
        in_second = jnp.where(routed & second, 1.0, 0.0)
        is_first = (line >= e * ROWS) & (line < e * ROWS + CAP)
        is_second = (line >= e * ROWS + CAP) & (line < (e + 1) * ROWS)
        listed = jnp.where(is_first, in_first, jnp.where(is_second, in_second, listed))
        weights = jnp.where(is_first | is_second, total, weights)
    before = lax.broadcasted_iota(jnp.int32, (count, count), 0)
    here = lax.broadcasted_iota(jnp.int32, (count, count), 1)
    upto = jnp.where(before <= here, 1.0, 0.0).astype(BF16)
    place = mm(listed.astype(BF16), upto, NN)
    wanted = (line % CAP + 1).astype(F32)
    picked = jnp.where((listed > 0.0) & (place == wanted), 1.0, 0.0)
    column = jnp.sum(picked * weights, axis=1, keepdims=True)
    for e in range(experts):
        picks[e] = rows_of(picked, e * ROWS)
    picked = picked.astype(BF16)
    for copy in copies[4:]:
        copy.wait()
    for s in range(groups):
        cut = slice(s * depth, (s + 1) * depth)
        token_rows = mm(picked, tokens[:, cut], NN)
        cot_rows = mm(picked, cots[:, cut], NN) * column
        parts = []
        for e in range(experts):
            parts += [rows_of(token_rows, e * ROWS), rows_of(cot_rows, e * ROWS)]
        slices[s] = jnp.concatenate(parts, axis=0).astype(BF16)
    for k in range(groups):
        outs[k][...] = slices[me[0] ^ k]


def weights_kernel(first, scale_gate, scale_up, scale_down, after, gate, up, down, gate_up, down_out):
    del after
    depth, hid = gate.shape
    step = math.gcd(depth, BLOCK)
    for i in range(depth // step):
        block = (first[0] + i * step) // BLOCK
        for h in range(hid // BLOCK):
            at = (slice(i * step, (i + 1) * step), slice(h * BLOCK, (h + 1) * BLOCK))
            to = slice(hid + h * BLOCK, hid + (h + 1) * BLOCK)
            gate_up[at] = (gate[at].astype(F32) * scale_gate[h, block]).astype(BF16)
            gate_up[at[0], to] = (up[at].astype(F32) * scale_up[h, block]).astype(BF16)
    lane = lax.broadcasted_iota(jnp.int32, (1, depth), 1)
    start = first[0] // BLOCK
    last = scale_down.shape[1] - 1
    for h in range(hid // BLOCK):
        spread = jnp.zeros((1, depth), F32) + scale_down[h, start]
        for j in range(1, depth // BLOCK + 2):
            block = jnp.minimum(start + j, last)
            spread = jnp.where(lane >= (start + j) * BLOCK - first[0], scale_down[h, block], spread)
        at = slice(h * BLOCK, (h + 1) * BLOCK)
        down_out[at, :] = (down[at, :].astype(F32) * spread).astype(BF16)


def token_part(chunks):
    return jnp.concatenate([c[: c.shape[0] // 2, :] for c in chunks], axis=0)


def cot_part(chunks):
    return jnp.concatenate([c[c.shape[0] // 2 :, :] for c in chunks], axis=0)


def partial_kernel(groups, chips, *refs):
    chunks, weights, outs = refs[:chips], refs[chips : chips + 4], refs[chips + 4 :]
    tokens, cots = token_part(chunks), cot_part(chunks)
    hid = weights[1].shape[0]
    for half in range(2):
        gate_up, down = weights[2 * half], weights[2 * half + 1]
        for product, at in (
            (mm(tokens, gate_up[...], NN), 0),
            (mm(cots, down[...], NT), 2 * hid),
        ):
            cut = slice(3 * hid * half + at, 3 * hid * half + at + product.shape[1])
            for k in range(groups):
                rows = [rows_of(product, (c * groups + k) * ROWS) for c in range(chips)]
                outs[k][:, cut] = jnp.concatenate(rows, axis=0).astype(outs[k].dtype)


def act_kernel(groups, *refs):
    parts, out = refs[:groups], refs[groups]
    hid = out.shape[1] // 6
    for half in range(2):
        values = []
        for i in range(3):
            cut = slice((3 * half + i) * hid, (3 * half + i + 1) * hid)
            total = parts[0][:, cut]
            for part in parts[1:]:
                total = total + part[:, cut].astype(F32)
            values.append(total)
        a, b, dh = values
        sig = jax.nn.sigmoid(a)
        swish = a * sig
        results = (dh * b * sig * (1.0 + a * (1.0 - sig)), dh * swish, swish * b)
        for i, result in enumerate(results):
            cut = slice((3 * half + i) * hid, (3 * half + i + 1) * hid)
            out[:, cut] = result.astype(BF16)


def dx_kernel(near, chips, *refs):
    acts, weights, outs = refs[:near], refs[near : near + 4], refs[near + 4 :]
    own, other, own_pair, other_pair = weights
    depth, hid = own.shape[0], own.shape[1] // 2
    act = jnp.concatenate([a[...] for a in acts], axis=0)
    first, second = act[:, : 2 * hid], act[:, 3 * hid : 5 * hid]
    for half, (left, right) in enumerate(((own, other), (own_pair, other_pair))):
        dx = mm(first, left[...], NT) + mm(second, right[...], NT)
        for c in range(chips):
            rows = [rows_of(dx, (k * chips + c) * ROWS) for k in range(near)]
            cut = slice(half * depth, (half + 1) * depth)
            outs[c][:, cut] = jnp.concatenate(rows, axis=0).astype(outs[c].dtype)


def share_kernel(groups, chips, *refs):
    acts, own, other = refs[:groups], refs[groups], refs[groups + 1]
    hid = own.shape[1] // 3
    act = jnp.concatenate([a[...] for a in acts], axis=0)
    own[...] = regroup(act[:, : 3 * hid], groups, chips)
    other[...] = regroup(act[:, 3 * hid :], groups, chips)


def collect_kernel(near, chips, *refs):
    parts, outs = refs[len(refs) - chips - near : len(refs) - near], refs[len(refs) - near :]
    sums = []
    for first in range(0, chips, CHIPS):
        total = parts[first][...].astype(F32)
        for part in parts[first + 1 : first + CHIPS]:
            total = total + part[...].astype(F32)
        sums.append(total)
    for k in range(near):
        rows = [rows_of(total, k * ROWS) for total in sums]
        outs[k][...] = jnp.concatenate(rows, axis=0).astype(BF16)


def place_kernel(groups, experts, me, home, *refs):
    near = groups // 2
    parts, picks, out, slices = refs[:near], refs[near], refs[near + 1], refs[near + 2]
    depth = parts[0].shape[1] // 2
    for k in range(near):
        for half in range(2):
            slices[me[0] ^ (2 * k + half)] = parts[k][:, half * depth : (half + 1) * depth].astype(F32)
    for s in range(groups):
        total = jnp.zeros((out.shape[0], depth), F32)
        for x in range(experts):
            rows = slices[s, x * ROWS : (x + 1) * ROWS, :].astype(BF16)
            total = total + mm(picks[home[0] ^ x].astype(BF16), rows, TN)
        out[:, s * depth : (s + 1) * depth] = total.astype(BF16)


def regroup(act, groups, chips):
    wide = act.astype(F32)
    rows = [rows_of(wide, (k * chips + c) * ROWS) for c in range(chips) for k in range(groups)]
    return jnp.concatenate(rows, axis=0).astype(BF16)


def grads_kernel(chips, *refs):
    own, other, acts = refs[:chips], refs[chips : 2 * chips], refs[2 * chips : 2 * chips + 2]
    grad_gate, grad_up, grad_down = refs[2 * chips + 2 :]
    hid = grad_gate.shape[1]
    tokens = jnp.concatenate([token_part(own), token_part(other)], axis=0)
    cots = jnp.concatenate([cot_part(own), cot_part(other)], axis=0)
    act = jnp.concatenate([a[...] for a in acts], axis=0)
    grad_gate[...] = mm(tokens, act[:, :hid], TN).astype(BF16)
    grad_up[...] = mm(tokens, act[:, hid : 2 * hid], TN).astype(BF16)
    grad_down[...] = mm(act[:, 2 * hid :], cots, TN).astype(BF16)


def chunk_of(parts, experts, slot):
    blocks = [p.reshape(experts, 2, ROWS, p.shape[1]) for p in parts]
    if experts == 1:
        blocks = [b[0] for b in blocks]
    else:
        blocks = [lax.dynamic_index_in_dim(b, slot, 0, keepdims=False) for b in blocks]
    return jnp.concatenate([b[0] for b in blocks] + [b[1] for b in blocks], axis=0)


def on_device(
    tokens,
    cotangent,
    route_weight,
    expert_ids,
    live_tokens,
    replica_plan,
    w_gate,
    w_up,
    w_down,
    scale_gate,
    scale_up,
    scale_down,
):
    members, groups = lax.axis_size("expert"), lax.axis_size("dp")
    experts, chips, near = members // HSH, members // 2, groups // 2
    count, width = tokens.shape
    depth, hid = w_gate.shape
    group, member = lax.axis_index("dp"), lax.axis_index("expert")
    me = jnp.reshape(group, (1,))
    home = jnp.reshape(member // HSH, (1,))
    rows = groups * chips * ROWS

    *sent, picks = call(
        functools.partial(route_kernel, groups, experts),
        [shape((2 * ROWS * experts, depth))] * groups + [shape((experts, ROWS, count), F32)],
        (me,),
        (),
        far=(live_tokens, replica_plan, expert_ids.T, route_weight.T, tokens, cotangent),
        scratch=[
            pltpu.SMEM(live_tokens.shape, jnp.int32),
            pltpu.SMEM(replica_plan.shape, jnp.int32),
            pltpu.VMEM(expert_ids.shape[::-1], jnp.int32),
            pltpu.VMEM(route_weight.shape[::-1], F32),
            pltpu.VMEM(tokens.shape, BF16),
            pltpu.VMEM(cotangent.shape, BF16),
            pltpu.VMEM((groups, 2 * ROWS * experts, depth), BF16),
            pltpu.SemaphoreType.DMA((6,)),
        ],
        flops=4 * count * experts * ROWS * width,
        name="route",
    )
    parts = [sent[0]] + [swap(sent[k], "dp", k) for k in range(1, groups)]
    chunks = [chunk_of(parts, experts, member // HSH)]
    for c in range(1, chips):
        out = chunks[0] if experts == 1 else chunk_of(parts, experts, (member ^ (2 * c)) // HSH)
        chunks.append(swap(out, "expert", 2 * c))

    gate_up, down = call(
        weights_kernel,
        [shape((depth, 2 * hid)), shape((hid, depth))],
        (me * depth, scale_gate.T, scale_up.T, scale_down),
        (w_gate, w_up, w_down),
        far=(chunks[0],),
        flops=6 * depth * hid,
        name="weights",
    )
    other_gate_up, other_down = swap(gate_up, "expert", 1), swap(down, "expert", 1)
    gate_up_pair = swap(gate_up, "dp", 1)

    partial = call(
        functools.partial(partial_kernel, groups, chips),
        [shape((chips * ROWS, 6 * hid), F32 if k == 0 else BF16) for k in range(groups)],
        (),
        (*chunks, gate_up, down, other_gate_up, other_down),
        flops=12 * rows * depth * hid,
        name="partial",
    )
    summands = [partial[0]] + [swap(partial[k], "dp", k) for k in range(1, groups)]
    other_chunks = [swap(c, "expert", 1) for c in chunks]
    other_gate_up_pair = swap(gate_up_pair, "expert", 1)

    (act,) = call(
        functools.partial(act_kernel, groups),
        [shape((chips * ROWS, 6 * hid))],
        (),
        summands,
        flops=40 * chips * ROWS * hid,
        name="activations",
    )
    acts = [act] + [swap(act, "dp", k) for k in range(1, groups)]
    dx = call(
        functools.partial(dx_kernel, near, chips),
        [shape((near * ROWS, 2 * depth), F32 if c == 0 else BF16) for c in range(chips)],
        (),
        (*acts[::2], gate_up, other_gate_up, gate_up_pair, other_gate_up_pair),
        flops=8 * rows * depth * hid,
        name="dx",
    )
    returned = [dx[0]] + [swap(dx[c], "expert", 2 * c) for c in range(1, chips)]

    act_own, act_out = call(
        functools.partial(share_kernel, groups, chips),
        [shape((rows, 3 * hid))] * 2,
        (),
        acts,
        name="share",
    )
    act_other = swap(act_out, "expert", 1)
    grads = call(
        functools.partial(grads_kernel, chips),
        [shape((depth, hid)), shape((depth, hid)), shape((hid, depth))],
        (),
        (*chunks, *other_chunks, act_own, act_other),
        flops=12 * rows * depth * hid,
        name="gradients",
    )
    home_rows = call(
        functools.partial(collect_kernel, near, chips),
        [shape((experts * ROWS, 2 * depth))] * near,
        (),
        returned,
        far=(grads[0],),
        flops=rows * depth,
        name="collect",
    )
    placed = [home_rows[0]] + [swap(home_rows[k], "dp", 2 * k) for k in range(1, near)]
    (d_tokens,) = call(
        functools.partial(place_kernel, groups, experts),
        [shape((count, width))],
        (me, home),
        (*placed, picks),
        scratch=[pltpu.VMEM((groups, experts * ROWS, depth), F32)],
        flops=2 * count * experts * ROWS * width,
        name="place",
    )
    return (d_tokens, *grads)


def solution(mesh):
    return jax.shard_map(
        on_device,
        mesh=mesh,
        in_specs=(
            P(("dp", "expert"), None),
            P(("dp", "expert"), None),
            P(("dp", "expert"), None),
            P(("dp", "expert"), None),
            P(("dp", "expert")),
            P(("dp", "expert"), None),
            P("dp", "expert"),
            P("dp", "expert"),
            P("expert", "dp"),
            P(None, "expert"),
            P(None, "expert"),
            P("expert", None),
        ),
        out_specs=(
            P(("dp", "expert"), None),
            P("dp", "expert"),
            P("dp", "expert"),
            P("expert", "dp"),
        ),
        check_vma=False,
    )
```

```python
import functools
import math

import jax
import jax.numpy as jnp
from jax import lax
from jax.experimental import pallas as pl
from jax.experimental.pallas import tpu as pltpu
from jax.sharding import PartitionSpec as P

HSH = 8
CAP = 4
ROWS = 2 * CAP
BLOCK = 128
CHIPS = HSH // 2
BF16 = jnp.bfloat16
F32 = jnp.float32
VMEM_BYTES = 40 * 1024 * 1024
ROUTE_VMEM_BYTES = 62 * 1024 * 1024

NN = (((1,), (0,)), ((), ()))
NT = (((1,), (1,)), ((), ()))
TN = (((0,), (0,)), ((), ()))


def mm(a, b, dims):
    return lax.dot_general(a, b, dims, preferred_element_type=F32)


def call(kernel, outs, scalars, arrays, hbm=(), after=(), scratch=(), flops=0, name=None, far_out=False, limit=VMEM_BYTES):
    moved = sum(math.prod(x.shape) * x.dtype.itemsize for x in (*hbm, *arrays, *outs))
    count = len(scalars) + len(hbm)

    def body(*refs):
        kernel(*refs[:count], *refs[count + len(after) :])

    return pl.pallas_call(
        body,
        out_shape=outs,
        in_specs=[pl.BlockSpec(memory_space=pltpu.SMEM)] * len(scalars)
        + [pl.BlockSpec(memory_space=pltpu.HBM)] * len(hbm)
        + [pl.BlockSpec(memory_space=pltpu.VMEM)] * len(after)
        + [pl.BlockSpec(memory_space=pltpu.VMEM)] * len(arrays),
        out_specs=[pl.BlockSpec(memory_space=pltpu.HBM if far_out else pltpu.VMEM)] * len(outs),
        scratch_shapes=list(scratch),
        compiler_params=pltpu.CompilerParams(vmem_limit_bytes=limit),
        cost_estimate=pl.CostEstimate(flops=flops, bytes_accessed=moved, transcendentals=0),
        name=name,
    )(*scalars, *hbm, *after, *arrays)


def fetch(sources, targets, sems):
    copies = [pltpu.make_async_copy(s, t, sems.at[i]) for i, (s, t) in enumerate(zip(sources, targets))]
    for copy in copies:
        copy.start()
    return copies


def shape(dims, dtype=BF16):
    return jax.ShapeDtypeStruct(dims, dtype)


def swap(x, axis, k):
    return lax.ppermute(x, axis, [(i, i ^ k) for i in range(lax.axis_size(axis))])


def rows_of(value, first, count=ROWS):
    return value[first : first + count]


def route_kernel(groups, experts, me, ids_in, weight_in, tokens_in, cots_in, live, plan, *rest):
    outs, picks, scratch = rest[:groups], rest[groups], rest[groups + 1 :]
    ids, weight, tokens, cots, slices, sems = scratch
    count, width = tokens.shape
    depth = width // groups
    small = fetch((ids_in, weight_in), (ids, weight), sems)
    large = []
    if depth % BLOCK == 0:
        cuts = [(slice(None), pl.ds(i * depth, depth)) for i in range(groups)]
    else:
        cuts = [(slice(None), slice(None))]
    for i, cut in enumerate(cuts):
        for source, target, sem in ((tokens_in, tokens, 2 + i), (cots_in, cots, 2 + groups + i)):
            large.append(pltpu.make_async_copy(source.at[cut], target.at[cut], sems.at[sem]))
            large[-1].start()
    for copy in small:
        copy.wait()
    lists = experts * ROWS
    slot = lax.broadcasted_iota(jnp.int32, (1, count), 1)
    line = lax.broadcasted_iota(jnp.int32, (lists, count), 0)
    alive = slot < live[...]
    odd = slot % 2 == 1
    listed = jnp.zeros((lists, count), F32)
    weights = jnp.zeros((lists, count), F32)
    for e in range(experts):
        match = ids[...] == e
        routed = (jnp.sum(jnp.where(match, 1.0, 0.0), axis=0, keepdims=True) > 0.0) & alive
        total = jnp.sum(jnp.where(match, weight[...], 0.0), axis=0, keepdims=True)
        second = odd & (plan[:, e : e + 1] == 1)
        in_first = jnp.where(routed & ~second, 1.0, 0.0)
        in_second = jnp.where(routed & second, 1.0, 0.0)
        is_first = (line >= e * ROWS) & (line < e * ROWS + CAP)
        is_second = (line >= e * ROWS + CAP) & (line < (e + 1) * ROWS)
        listed = jnp.where(is_first, in_first, jnp.where(is_second, in_second, listed))
        weights = jnp.where(is_first | is_second, total, weights)
    before = lax.broadcasted_iota(jnp.int32, (count, count), 0)
    here = lax.broadcasted_iota(jnp.int32, (count, count), 1)
    upto = jnp.where(before <= here, 1.0, 0.0).astype(BF16)
    place = mm(listed.astype(BF16), upto, NN)
    wanted = (line % CAP + 1).astype(F32)
    picked = jnp.where((listed > 0.0) & (place == wanted), 1.0, 0.0)
    column = jnp.sum(picked * weights, axis=1, keepdims=True)
    for e in range(experts):
        picks[e] = rows_of(picked, e * ROWS)
    picked = picked.astype(BF16)
    for s in range(groups):
        for copy in large[2 * s : 2 * s + 2]:
            copy.wait()
        cut = slice(s * depth, (s + 1) * depth)
        token_rows = mm(picked, tokens[:, cut], NN)
        cot_rows = mm(picked, cots[:, cut], NN) * column
        parts = []
        for e in range(experts):
            parts += [rows_of(token_rows, e * ROWS), rows_of(cot_rows, e * ROWS)]
        slices[s] = jnp.concatenate(parts, axis=0).astype(BF16)
    for k in range(groups):
        outs[k][...] = slices[me[0] ^ k]


def weights_kernel(first, scale_gate, scale_up, scale_down, gate, up, down, gate_up, down_out, packed):
    depth, hid = gate.shape
    step = math.gcd(depth, BLOCK)
    for i in range(depth // step):
        block = (first[0] + i * step) // BLOCK
        for h in range(hid // BLOCK):
            at = (slice(i * step, (i + 1) * step), slice(h * BLOCK, (h + 1) * BLOCK))
            to = (at[0], slice(hid + h * BLOCK, hid + (h + 1) * BLOCK))
            for out in (gate_up, packed):
                out[at] = (gate[at].astype(F32) * scale_gate[h, block]).astype(BF16)
                out[to] = (up[at].astype(F32) * scale_up[h, block]).astype(BF16)
    lane = lax.broadcasted_iota(jnp.int32, (1, depth), 1)
    start = first[0] // BLOCK
    last = scale_down.shape[1] - 1
    for h in range(hid // BLOCK):
        spread = jnp.zeros((1, depth), F32) + scale_down[h, start]
        for j in range(1, depth // BLOCK + 2):
            block = jnp.minimum(start + j, last)
            spread = jnp.where(lane >= (start + j) * BLOCK - first[0], scale_down[h, block], spread)
        at = slice(h * BLOCK, (h + 1) * BLOCK)
        value = (down[at, :].astype(F32) * spread).astype(BF16)
        down_out[at, :] = value
        for i, (begin, end) in enumerate(pieces(depth, 2 * hid)):
            top = depth + i * hid + h * BLOCK
            packed[top : top + BLOCK, : end - begin] = value[:, begin:end]


def pieces(length, size):
    return [(i, min(i + size, length)) for i in range(0, length, size)]


def token_part(chunks):
    return jnp.concatenate([c[: c.shape[0] // 2, :] for c in chunks], axis=0)


def cot_part(chunks):
    return jnp.concatenate([c[c.shape[0] // 2 :, :] for c in chunks], axis=0)


def partial_kernel(groups, chips, *refs):
    chunks, (gate_up, down, packed), outs = refs[:chips], refs[chips : chips + 3], refs[chips + 3 :]
    tokens, cots = token_part(chunks), cot_part(chunks)
    outs[groups][...] = jnp.concatenate([tokens, cots], axis=0)
    hid, depth = down.shape
    dh = 0.0
    for i, (begin, end) in enumerate(pieces(depth, 2 * hid)):
        top = depth + i * hid
        dh = dh + mm(cots[:, begin:end], packed[top : top + hid, : end - begin], NT)
    products = (
        (mm(tokens, gate_up[...], NN), 0),
        (mm(cots, down[...], NT), 2 * hid),
        (mm(tokens, packed[:depth, :], NN), 3 * hid),
        (dh, 5 * hid),
    )
    for product, at in products:
        cut = slice(at, at + product.shape[1])
        for k in range(groups):
            rows = [rows_of(product, (c * groups + k) * ROWS) for c in range(chips)]
            outs[k][:, cut] = jnp.concatenate(rows, axis=0).astype(outs[k].dtype)


def act_kernel(groups, *refs):
    parts, out = refs[:groups], refs[groups]
    hid = out.shape[1] // 6
    for half in range(2):
        values = []
        for i in range(3):
            cut = slice((3 * half + i) * hid, (3 * half + i + 1) * hid)
            total = parts[0][:, cut]
            for part in parts[1:]:
                total = total + part[:, cut].astype(F32)
            values.append(total)
        a, b, dh = values
        sig = jax.nn.sigmoid(a)
        swish = a * sig
        results = (dh * b * sig * (1.0 + a * (1.0 - sig)), dh * swish, swish * b)
        for i, result in enumerate(results):
            cut = slice((3 * half + i) * hid, (3 * half + i + 1) * hid)
            out[:, cut] = result.astype(BF16)


def dx_kernel(groups, chips, *refs):
    acts, (own, other), outs = refs[:groups], refs[groups : groups + 2], refs[groups + 2 :]
    depth, hid = own.shape[0], own.shape[1] // 2
    act = jnp.concatenate([a[...] for a in acts], axis=0)
    dx = mm(act[:, : 2 * hid], own[...], NT)
    dx = dx + mm(act[:, 3 * hid : 5 * hid], other[:depth, :], NT)
    for c in range(chips):
        rows = [rows_of(dx, (k * chips + c) * ROWS) for k in range(groups)]
        outs[c][...] = jnp.concatenate(rows, axis=0).astype(outs[c].dtype)
    outs[chips][...] = regroup(act[:, : 3 * hid], groups, chips)
    outs[chips + 1][...] = regroup(act[:, 3 * hid :], groups, chips)


def collect_kernel(groups, chips, *refs):
    parts, outs = refs[:chips], refs[chips:]
    sums = []
    for first in range(0, chips, CHIPS):
        total = parts[first][...].astype(F32)
        for part in parts[first + 1 : first + CHIPS]:
            total = total + part[...].astype(F32)
        sums.append(total)
    for k in range(groups):
        rows = [rows_of(total, k * ROWS) for total in sums]
        outs[k][...] = jnp.concatenate(rows, axis=0).astype(BF16)


def place_kernel(groups, experts, me, home, *refs):
    parts, (picks, out, slices, result, sems) = refs[:groups], refs[groups:]
    depth = parts[0].shape[1]
    copies = []
    for k in range(groups):
        slices[me[0] ^ k] = parts[k][...].astype(F32)
    for s in range(groups):
        total = jnp.zeros((out.shape[0], depth), F32)
        for x in range(experts):
            rows = slices[s, x * ROWS : (x + 1) * ROWS, :].astype(BF16)
            total = total + mm(picks[home[0] ^ x].astype(BF16), rows, TN)
        cut = slice(s * depth, (s + 1) * depth)
        result[:, cut] = total.astype(BF16)
        if depth % BLOCK == 0:
            copies.append(pltpu.make_async_copy(result.at[:, cut], out.at[:, cut], sems.at[s]))
            copies[-1].start()
    if not copies:
        copies.append(pltpu.make_async_copy(result, out, sems.at[0]))
        copies[-1].start()
    for copy in copies:
        copy.wait()


def regroup(act, groups, chips):
    wide = act.astype(F32)
    rows = [rows_of(wide, (k * chips + c) * ROWS) for c in range(chips) for k in range(groups)]
    return jnp.concatenate(rows, axis=0).astype(BF16)


def grads_kernel(own, other, act_own, act_other, grad_gate, grad_up, grad_down, token):
    hid, half = grad_gate.shape[1], own.shape[0] // 2
    acts = (act_own, act_other)
    tokens = jnp.concatenate([own[:half, :], other[:half, :]], axis=0)
    cots = jnp.concatenate([own[half:, :], other[half:, :]], axis=0)
    act = jnp.concatenate([a[...] for a in acts], axis=0)
    grad_gate[...] = mm(tokens, act[:, :hid], TN).astype(BF16)
    grad_up[...] = mm(tokens, act[:, hid : 2 * hid], TN).astype(BF16)
    grad_down[...] = mm(act[:, 2 * hid :], cots, TN).astype(BF16)
    token[...] = jnp.zeros_like(token)


def chunk_of(parts, experts, slot):
    blocks = [p.reshape(experts, 2, ROWS, p.shape[1]) for p in parts]
    if experts == 1:
        blocks = [b[0] for b in blocks]
    else:
        blocks = [lax.dynamic_index_in_dim(b, slot, 0, keepdims=False) for b in blocks]
    return jnp.concatenate([b[0] for b in blocks] + [b[1] for b in blocks], axis=0)


def on_device(
    tokens,
    cotangent,
    route_weight,
    expert_ids,
    live_tokens,
    replica_plan,
    w_gate,
    w_up,
    w_down,
    scale_gate,
    scale_up,
    scale_down,
):
    members, groups = lax.axis_size("expert"), lax.axis_size("dp")
    experts, chips = members // HSH, members // 2
    count, width = tokens.shape
    depth, hid = w_gate.shape
    group, member = lax.axis_index("dp"), lax.axis_index("expert")
    me = jnp.reshape(group, (1,))
    home = jnp.reshape(member // HSH, (1,))
    rows = groups * chips * ROWS

    *sent, picks = call(
        functools.partial(route_kernel, groups, experts),
        [shape((2 * ROWS * experts, depth))] * groups + [shape((experts, ROWS, count), F32)],
        (me,),
        (live_tokens.reshape(1, 1), replica_plan),
        hbm=(expert_ids.T, route_weight.T, tokens, cotangent),
        scratch=[
            pltpu.VMEM(expert_ids.shape[::-1], jnp.int32),
            pltpu.VMEM(route_weight.shape[::-1], F32),
            pltpu.VMEM(tokens.shape, BF16),
            pltpu.VMEM(cotangent.shape, BF16),
            pltpu.VMEM((groups, 2 * ROWS * experts, depth), BF16),
            pltpu.SemaphoreType.DMA((2 + 2 * groups,)),
        ],
        flops=4 * count * experts * ROWS * width,
        limit=ROUTE_VMEM_BYTES,
        name="route",
    )
    parts = [sent[0]] + [swap(sent[k], "dp", k) for k in range(1, groups)]
    chunks = [chunk_of(parts, experts, member // HSH)]
    for c in range(1, chips):
        out = chunks[0] if experts == 1 else chunk_of(parts, experts, (member ^ (2 * c)) // HSH)
        chunks.append(swap(out, "expert", 2 * c))

    tall = depth + hid * len(pieces(depth, 2 * hid))
    gate_up, down, packed = call(
        weights_kernel,
        [shape((depth, 2 * hid)), shape((hid, depth)), shape((tall, 2 * hid))],
        (me * depth, scale_gate.T, scale_up.T, scale_down),
        (w_gate, w_up, w_down),
        after=(parts[1],),
        flops=6 * depth * hid,
        name="weights",
    )
    other = swap(packed, "expert", 1)

    *partial, own_rows = call(
        functools.partial(partial_kernel, groups, chips),
        [shape((chips * ROWS, 6 * hid), F32 if k == 0 else BF16) for k in range(groups)]
        + [shape((2 * rows, depth))],
        (),
        (*chunks, gate_up, down, other),
        flops=12 * rows * depth * hid,
        name="partial",
    )
    other_rows = swap(own_rows, "expert", 1)
    summands = [partial[0]] + [swap(partial[k], "dp", k) for k in range(1, groups)]
    (act,) = call(
        functools.partial(act_kernel, groups),
        [shape((chips * ROWS, 6 * hid))],
        (),
        summands,
        flops=40 * chips * ROWS * hid,
        name="activations",
    )
    acts = [act] + [swap(act, "dp", k) for k in range(1, groups)]
    *dx, act_own, act_out = call(
        functools.partial(dx_kernel, groups, chips),
        [shape((groups * ROWS, depth), F32 if c == 0 else BF16) for c in range(chips)]
        + [shape((rows, 3 * hid))] * 2,
        (),
        (*acts, gate_up, other),
        flops=8 * rows * depth * hid,
        name="dx",
    )
    returned = [dx[0]] + [swap(dx[c], "expert", 2 * c) for c in range(1, chips)]
    home_rows = call(
        functools.partial(collect_kernel, groups, chips),
        [shape((experts * ROWS, depth))] * groups,
        (),
        returned,
        flops=rows * depth,
        name="collect",
    )
    placed = [home_rows[0]] + [swap(home_rows[k], "dp", k) for k in range(1, groups)]
    act_other = swap(act_out, "expert", 1)
    *grads, done = call(
        grads_kernel,
        [shape((depth, hid)), shape((depth, hid)), shape((hid, depth)), shape((8, BLOCK), F32)],
        (),
        (own_rows, other_rows, act_own, act_other),
        flops=12 * rows * depth * hid,
        name="gradients",
    )
    (d_tokens,) = call(
        functools.partial(place_kernel, groups, experts),
        [shape((count, width))],
        (me, home),
        (*placed, picks),
        after=(done,),
        far_out=True,
        scratch=[
            pltpu.VMEM((groups, experts * ROWS, depth), F32),
            pltpu.VMEM((count, width), BF16),
            pltpu.SemaphoreType.DMA((groups,)),
        ],
        flops=2 * count * experts * ROWS * width,
        name="place",
    )
    return (d_tokens, *grads)


def solution(mesh):
    return jax.shard_map(
        on_device,
        mesh=mesh,
        in_specs=(
            P(("dp", "expert"), None),
            P(("dp", "expert"), None),
            P(("dp", "expert"), None),
            P(("dp", "expert"), None),
            P(("dp", "expert")),
            P(("dp", "expert"), None),
            P("dp", "expert"),
            P("dp", "expert"),
            P("expert", "dp"),
            P(None, "expert"),
            P(None, "expert"),
            P("expert", None),
        ),
        out_specs=(
            P(("dp", "expert"), None),
            P("dp", "expert"),
            P("dp", "expert"),
            P("expert", "dp"),
        ),
        check_vma=False,
    )
```

```python
import functools
import math

import jax
import jax.numpy as jnp
from jax import lax
from jax.experimental import pallas as pl
from jax.experimental.pallas import tpu as pltpu
from jax.sharding import PartitionSpec as P

HSH = 8
CAP = 4
ROWS = 2 * CAP
BLOCK = 128
CHIPS = HSH // 2
BF16 = jnp.bfloat16
F32 = jnp.float32
VMEM_BYTES = 40 * 1024 * 1024
ROUTE_VMEM_BYTES = 61 * 1024 * 1024

NN = (((1,), (0,)), ((), ()))
NT = (((1,), (1,)), ((), ()))
TN = (((0,), (0,)), ((), ()))


def mm(a, b, dims):
    return lax.dot_general(a, b, dims, preferred_element_type=F32)


def call(kernel, outs, scalars, arrays, hbm=(), after=(), scratch=(), flops=0, name=None, far_out=False, limit=VMEM_BYTES):
    moved = sum(math.prod(x.shape) * x.dtype.itemsize for x in (*hbm, *arrays, *outs))
    count = len(scalars) + len(hbm)

    def body(*refs):
        kernel(*refs[:count], *refs[count + len(after) :])

    return pl.pallas_call(
        body,
        out_shape=outs,
        in_specs=[pl.BlockSpec(memory_space=pltpu.SMEM)] * len(scalars)
        + [pl.BlockSpec(memory_space=pltpu.HBM)] * len(hbm)
        + [pl.BlockSpec(memory_space=pltpu.VMEM)] * len(after)
        + [pl.BlockSpec(memory_space=pltpu.VMEM)] * len(arrays),
        out_specs=[pl.BlockSpec(memory_space=pltpu.HBM if far_out else pltpu.VMEM)] * len(outs),
        scratch_shapes=list(scratch),
        compiler_params=pltpu.CompilerParams(vmem_limit_bytes=limit),
        cost_estimate=pl.CostEstimate(flops=flops, bytes_accessed=moved, transcendentals=0),
        name=name,
    )(*scalars, *hbm, *after, *arrays)


def fetch(sources, targets, sems):
    copies = [pltpu.make_async_copy(s, t, sems.at[i]) for i, (s, t) in enumerate(zip(sources, targets))]
    for copy in copies:
        copy.start()
    return copies


def shape(dims, dtype=BF16):
    return jax.ShapeDtypeStruct(dims, dtype)


def swap(x, axis, k):
    return lax.ppermute(x, axis, [(i, i ^ k) for i in range(lax.axis_size(axis))])


def rows_of(value, first, count=ROWS):
    return value[first : first + count]


def route_kernel(groups, experts, me, ids_in, weight_in, tokens_in, cots_in, live, plan, *rest):
    outs, picks, scratch = rest[:groups], rest[groups], rest[groups + 1 :]
    ids, weight, tokens, cots, slices, sems = scratch
    count, width = tokens.shape
    depth = width // groups
    small = fetch((ids_in, weight_in), (ids, weight), sems)
    large = []
    if depth % BLOCK == 0:
        cuts = [(slice(None), pl.ds(i * depth, depth)) for i in range(groups)]
    else:
        cuts = [(slice(None), slice(None))]
    for i, cut in enumerate(cuts):
        for source, target, sem in ((tokens_in, tokens, 2 + i), (cots_in, cots, 2 + groups + i)):
            large.append(pltpu.make_async_copy(source.at[cut], target.at[cut], sems.at[sem]))
            large[-1].start()
    for copy in small:
        copy.wait()
    lists = experts * ROWS
    slot = lax.broadcasted_iota(jnp.int32, (1, count), 1)
    line = lax.broadcasted_iota(jnp.int32, (lists, count), 0)
    alive = slot < live[...]
    odd = slot % 2 == 1
    listed = jnp.zeros((lists, count), F32)
    weights = jnp.zeros((lists, count), F32)
    for e in range(experts):
        match = ids[...] == e
        routed = (jnp.sum(jnp.where(match, 1.0, 0.0), axis=0, keepdims=True) > 0.0) & alive
        total = jnp.sum(jnp.where(match, weight[...], 0.0), axis=0, keepdims=True)
        second = odd & (plan[:, e : e + 1] == 1)
        in_first = jnp.where(routed & ~second, 1.0, 0.0)
        in_second = jnp.where(routed & second, 1.0, 0.0)
        is_first = (line >= e * ROWS) & (line < e * ROWS + CAP)
        is_second = (line >= e * ROWS + CAP) & (line < (e + 1) * ROWS)
        listed = jnp.where(is_first, in_first, jnp.where(is_second, in_second, listed))
        weights = jnp.where(is_first | is_second, total, weights)
    before = lax.broadcasted_iota(jnp.int32, (count, count), 0)
    here = lax.broadcasted_iota(jnp.int32, (count, count), 1)
    upto = jnp.where(before <= here, 1.0, 0.0).astype(BF16)
    place = mm(listed.astype(BF16), upto, NN)
    wanted = (line % CAP + 1).astype(F32)
    picked = jnp.where((listed > 0.0) & (place == wanted), 1.0, 0.0)
    column = jnp.sum(picked * weights, axis=1, keepdims=True)
    for e in range(experts):
        picks[e] = rows_of(picked, e * ROWS)
    picked = picked.astype(BF16)
    for s in range(groups):
        for copy in large[2 * s : 2 * s + 2]:
            copy.wait()
        cut = slice(s * depth, (s + 1) * depth)
        token_rows = mm(picked, tokens[:, cut], NN)
        cot_rows = mm(picked, cots[:, cut], NN) * column
        parts = []
        for e in range(experts):
            parts += [rows_of(token_rows, e * ROWS), rows_of(cot_rows, e * ROWS)]
        slices[s] = jnp.concatenate(parts, axis=0).astype(BF16)
    for k in range(groups):
        outs[k][...] = slices[me[0] ^ k]


def weights_kernel(first, scale_gate, scale_up, scale_down, gate, up, down, gate_up, down_out, packed):
    depth, hid = gate.shape
    step = math.gcd(depth, BLOCK)
    for i in range(depth // step):
        block = (first[0] + i * step) // BLOCK
        for h in range(hid // BLOCK):
            at = (slice(i * step, (i + 1) * step), slice(h * BLOCK, (h + 1) * BLOCK))
            to = (at[0], slice(hid + h * BLOCK, hid + (h + 1) * BLOCK))
            for out in (gate_up, packed):
                out[at] = (gate[at].astype(F32) * scale_gate[h, block]).astype(BF16)
                out[to] = (up[at].astype(F32) * scale_up[h, block]).astype(BF16)
    lane = lax.broadcasted_iota(jnp.int32, (1, depth), 1)
    start = first[0] // BLOCK
    last = scale_down.shape[1] - 1
    for h in range(hid // BLOCK):
        spread = jnp.zeros((1, depth), F32) + scale_down[h, start]
        for j in range(1, depth // BLOCK + 2):
            block = jnp.minimum(start + j, last)
            spread = jnp.where(lane >= (start + j) * BLOCK - first[0], scale_down[h, block], spread)
        at = slice(h * BLOCK, (h + 1) * BLOCK)
        value = (down[at, :].astype(F32) * spread).astype(BF16)
        down_out[at, :] = value
        for i, (begin, end) in enumerate(pieces(depth, 2 * hid)):
            top = depth + i * hid + h * BLOCK
            packed[top : top + BLOCK, : end - begin] = value[:, begin:end]


def pieces(length, size):
    return [(i, min(i + size, length)) for i in range(0, length, size)]


def token_part(chunks):
    return jnp.concatenate([c[: c.shape[0] // 2, :] for c in chunks], axis=0)


def cot_part(chunks):
    return jnp.concatenate([c[c.shape[0] // 2 :, :] for c in chunks], axis=0)


def partial_kernel(groups, chips, *refs):
    chunks, (gate_up, down, packed), outs = refs[:chips], refs[chips : chips + 3], refs[chips + 3 :]
    tokens, cots = token_part(chunks), cot_part(chunks)
    outs[groups][...] = jnp.concatenate([tokens, cots], axis=0)
    hid, depth = down.shape
    dh = 0.0
    for i, (begin, end) in enumerate(pieces(depth, 2 * hid)):
        top = depth + i * hid
        dh = dh + mm(cots[:, begin:end], packed[top : top + hid, : end - begin], NT)
    products = (
        (mm(tokens, gate_up[...], NN), 0),
        (mm(cots, down[...], NT), 2 * hid),
        (mm(tokens, packed[:depth, :], NN), 3 * hid),
        (dh, 5 * hid),
    )
    for product, at in products:
        cut = slice(at, at + product.shape[1])
        for k in range(groups):
            rows = [rows_of(product, (c * groups + k) * ROWS) for c in range(chips)]
            outs[k][:, cut] = jnp.concatenate(rows, axis=0).astype(outs[k].dtype)


def act_kernel(groups, chips, chip, *refs):
    parts, out, ordered = refs[:groups], refs[groups], refs[groups + 1]
    hid = out.shape[1] // 6
    for half in range(2):
        values = []
        for i in range(3):
            cut = slice((3 * half + i) * hid, (3 * half + i + 1) * hid)
            total = parts[0][:, cut]
            for part in parts[1:]:
                total = total + part[:, cut].astype(F32)
            values.append(total)
        a, b, dh = values
        sig = jax.nn.sigmoid(a)
        swish = a * sig
        results = (dh * b * sig * (1.0 + a * (1.0 - sig)), dh * swish, swish * b)
        for i, result in enumerate(results):
            cut = slice((3 * half + i) * hid, (3 * half + i + 1) * hid)
            for c in range(chips):
                ordered[chip[0] ^ c, :, cut] = rows_of(result, c * ROWS)
    out[...] = jnp.concatenate([ordered[c] for c in range(chips)], axis=0).astype(BF16)


def dx_kernel(groups, chips, me, *refs):
    acts, (own, other, out) = refs[:groups], refs[groups:]
    depth, hid = own.shape[0], own.shape[1] // 2
    act = jnp.concatenate([a[...] for a in acts], axis=0)
    dx = mm(act[:, : 2 * hid], own[...], NT)
    dx = dx + mm(act[:, 3 * hid : 5 * hid], other[:depth, :], NT)
    count = chips * ROWS
    for k in range(groups):
        out[me[0] ^ k] = dx[k * count : (k + 1) * count].astype(BF16)


def share_kernel(groups, chips, chip, *refs):
    acts, own, out, blocks = refs[:groups], refs[groups], refs[groups + 1], refs[groups + 2]
    hid = own.shape[1] // 3
    for half, target in enumerate((own, out)):
        for k in range(groups):
            wide = acts[k][:, 3 * hid * half : 3 * hid * (half + 1)].astype(F32)
            for c in range(chips):
                blocks[k * chips + c] = rows_of(wide, c * ROWS)
        order = [blocks[k * chips + (chip[0] ^ c)] for c in range(chips) for k in range(groups)]
        target[...] = jnp.concatenate(order, axis=0).astype(BF16)


def place_kernel(groups, experts, chips, returned, picks, after, out, result, sems):
    depth = returned.shape[2]
    copies = []
    for s in range(groups):
        total = jnp.zeros((out.shape[0], depth), F32)
        for e in range(experts):
            rows = jnp.zeros((ROWS, depth), F32)
            for c in range(CHIPS):
                rows = rows + returned[s * chips + e * CHIPS + c].astype(F32)
            total = total + mm(picks[e].astype(BF16), rows.astype(BF16), TN)
        cut = slice(s * depth, (s + 1) * depth)
        result[:, cut] = total.astype(BF16)
        if depth % BLOCK == 0:
            copies.append(pltpu.make_async_copy(result.at[:, cut], out.at[:, cut], sems.at[s]))
            copies[-1].start()
    if not copies:
        copies.append(pltpu.make_async_copy(result, out, sems.at[0]))
        copies[-1].start()
    for copy in copies:
        copy.wait()


def grads_kernel(own, other, act_own, act_other, grad_gate, grad_up, grad_down, token):
    hid, half = grad_gate.shape[1], own.shape[0] // 2
    acts = (act_own, act_other)
    tokens = jnp.concatenate([own[:half, :], other[:half, :]], axis=0)
    cots = jnp.concatenate([own[half:, :], other[half:, :]], axis=0)
    act = jnp.concatenate([a[...] for a in acts], axis=0)
    grad_gate[...] = mm(tokens, act[:, :hid], TN).astype(BF16)
    grad_up[...] = mm(tokens, act[:, hid : 2 * hid], TN).astype(BF16)
    grad_down[...] = mm(act[:, 2 * hid :], cots, TN).astype(BF16)
    token[...] = jnp.zeros_like(token)


def chunk_of(parts, experts, slot):
    blocks = [p.reshape(experts, 2, ROWS, p.shape[1]) for p in parts]
    if experts == 1:
        blocks = [b[0] for b in blocks]
    else:
        blocks = [lax.dynamic_index_in_dim(b, slot, 0, keepdims=False) for b in blocks]
    return jnp.concatenate([b[0] for b in blocks] + [b[1] for b in blocks], axis=0)


def on_device(
    tokens,
    cotangent,
    route_weight,
    expert_ids,
    live_tokens,
    replica_plan,
    w_gate,
    w_up,
    w_down,
    scale_gate,
    scale_up,
    scale_down,
):
    members, groups = lax.axis_size("expert"), lax.axis_size("dp")
    experts, chips = members // HSH, members // 2
    count, width = tokens.shape
    depth, hid = w_gate.shape
    group, member = lax.axis_index("dp"), lax.axis_index("expert")
    me = jnp.reshape(group, (1,))
    rows = groups * chips * ROWS
    chip = jnp.reshape(member // 2, (1,))

    *sent, picks = call(
        functools.partial(route_kernel, groups, experts),
        [shape((2 * ROWS * experts, depth))] * groups + [shape((experts, ROWS, count), F32)],
        (me,),
        (live_tokens.reshape(1, 1), replica_plan),
        hbm=(expert_ids.T, route_weight.T, tokens, cotangent),
        scratch=[
            pltpu.VMEM(expert_ids.shape[::-1], jnp.int32),
            pltpu.VMEM(route_weight.shape[::-1], F32),
            pltpu.VMEM(tokens.shape, BF16),
            pltpu.VMEM(cotangent.shape, BF16),
            pltpu.VMEM((groups, 2 * ROWS * experts, depth), BF16),
            pltpu.SemaphoreType.DMA((2 + 2 * groups,)),
        ],
        flops=4 * count * experts * ROWS * width,
        limit=ROUTE_VMEM_BYTES,
        name="route",
    )
    parts = [sent[0]] + [swap(sent[k], "dp", k) for k in range(1, groups)]
    chunks = [chunk_of(parts, experts, member // HSH)]
    for c in range(1, chips):
        out = chunks[0] if experts == 1 else chunk_of(parts, experts, (member ^ (2 * c)) // HSH)
        chunks.append(swap(out, "expert", 2 * c))

    tall = depth + hid * len(pieces(depth, 2 * hid))
    gate_up, down, packed = call(
        weights_kernel,
        [shape((depth, 2 * hid)), shape((hid, depth)), shape((tall, 2 * hid))],
        (me * depth, scale_gate.T, scale_up.T, scale_down),
        (w_gate, w_up, w_down),
        after=(parts[1],),
        flops=6 * depth * hid,
        name="weights",
    )
    other = swap(packed, "expert", 1)

    *partial, own_rows = call(
        functools.partial(partial_kernel, groups, chips),
        [shape((chips * ROWS, 6 * hid), F32 if k == 0 else BF16) for k in range(groups)]
        + [shape((2 * rows, depth))],
        (),
        (*chunks, gate_up, down, other),
        flops=12 * rows * depth * hid,
        name="partial",
    )
    other_rows = swap(own_rows, "expert", 1)
    summands = [partial[0]] + [swap(partial[k], "dp", k) for k in range(1, groups)]
    (act,) = call(
        functools.partial(act_kernel, groups, chips),
        [shape((chips * ROWS, 6 * hid))],
        (chip,),
        summands,
        scratch=[pltpu.VMEM((chips, ROWS, 6 * hid), F32)],
        flops=40 * chips * ROWS * hid,
        name="activations",
    )
    acts = [act] + [swap(act, "dp", k) for k in range(1, groups)]
    (dx,) = call(
        functools.partial(dx_kernel, groups, chips),
        [shape((groups, chips * ROWS, depth))],
        (me,),
        (*acts, gate_up, other),
        flops=8 * rows * depth * hid,
        name="dx",
    )
    act_own, act_out = call(
        functools.partial(share_kernel, groups, chips),
        [shape((rows, 3 * hid))] * 2,
        (chip,),
        acts,
        after=(dx,),
        scratch=[pltpu.VMEM((groups * chips, ROWS, 3 * hid), F32)],
        name="share",
    )
    dx = dx.reshape(groups * chips, ROWS, depth)
    same_core = [
        [g * members + 2 * c + core for g in range(groups) for c in range(chips)] for core in range(2)
    ]
    returned = lax.all_to_all(
        dx, ("dp", "expert"), split_axis=0, concat_axis=0, axis_index_groups=same_core, tiled=True
    )
    act_other = swap(act_out, "expert", 1)
    *grads, done = call(
        grads_kernel,
        [shape((depth, hid)), shape((depth, hid)), shape((hid, depth)), shape((8, BLOCK), F32)],
        (),
        (own_rows, other_rows, act_own, act_other),
        flops=12 * rows * depth * hid,
        name="gradients",
    )
    (d_tokens,) = call(
        functools.partial(place_kernel, groups, experts, chips),
        [shape((count, width))],
        (),
        (returned, picks, done),
        far_out=True,
        scratch=[pltpu.VMEM((count, width), BF16), pltpu.SemaphoreType.DMA((groups,))],
        flops=2 * count * experts * ROWS * width,
        name="place",
    )
    return (d_tokens, *grads)


def solution(mesh):
    return jax.shard_map(
        on_device,
        mesh=mesh,
        in_specs=(
            P(("dp", "expert"), None),
            P(("dp", "expert"), None),
            P(("dp", "expert"), None),
            P(("dp", "expert"), None),
            P(("dp", "expert")),
            P(("dp", "expert"), None),
            P("dp", "expert"),
            P("dp", "expert"),
            P("expert", "dp"),
            P(None, "expert"),
            P(None, "expert"),
            P("expert", None),
        ),
        out_specs=(
            P(("dp", "expert"), None),
            P("dp", "expert"),
            P("dp", "expert"),
            P("expert", "dp"),
        ),
        check_vma=False,
    )
```

```python
import functools
import math

import jax
import jax.numpy as jnp
from jax import lax
from jax.experimental import pallas as pl
from jax.experimental.pallas import tpu as pltpu
from jax.sharding import PartitionSpec as P

HSH = 8
CAP = 4
ROWS = 2 * CAP
BLOCK = 128
CHIPS = HSH // 2
BF16 = jnp.bfloat16
F32 = jnp.float32
VMEM_BYTES = 40 * 1024 * 1024
ROUTE_VMEM_BYTES = 61 * 1024 * 1024

NN = (((1,), (0,)), ((), ()))
NT = (((1,), (1,)), ((), ()))
TN = (((0,), (0,)), ((), ()))


def mm(a, b, dims):
    return lax.dot_general(a, b, dims, preferred_element_type=F32)


def call(kernel, outs, scalars, arrays, hbm=(), after=(), scratch=(), flops=0, name=None, far_out=False, limit=VMEM_BYTES):
    moved = sum(math.prod(x.shape) * x.dtype.itemsize for x in (*hbm, *arrays, *outs))
    count = len(scalars) + len(hbm)

    def body(*refs):
        kernel(*refs[:count], *refs[count + len(after) :])

    return pl.pallas_call(
        body,
        out_shape=outs,
        in_specs=[pl.BlockSpec(memory_space=pltpu.SMEM)] * len(scalars)
        + [pl.BlockSpec(memory_space=pltpu.HBM)] * len(hbm)
        + [pl.BlockSpec(memory_space=pltpu.VMEM)] * len(after)
        + [pl.BlockSpec(memory_space=pltpu.VMEM)] * len(arrays),
        out_specs=[pl.BlockSpec(memory_space=pltpu.HBM if far_out else pltpu.VMEM)] * len(outs),
        scratch_shapes=list(scratch),
        compiler_params=pltpu.CompilerParams(vmem_limit_bytes=limit),
        cost_estimate=pl.CostEstimate(flops=flops, bytes_accessed=moved, transcendentals=0),
        name=name,
    )(*scalars, *hbm, *after, *arrays)


def fetch(sources, targets, sems):
    copies = [pltpu.make_async_copy(s, t, sems.at[i]) for i, (s, t) in enumerate(zip(sources, targets))]
    for copy in copies:
        copy.start()
    return copies


def shape(dims, dtype=BF16):
    return jax.ShapeDtypeStruct(dims, dtype)


def swap(x, axis, k):
    return lax.ppermute(x, axis, [(i, i ^ k) for i in range(lax.axis_size(axis))])


def rows_of(value, first, count=ROWS):
    return value[first : first + count]


def route_kernel(groups, experts, ids_in, weight_in, tokens_in, cots_in, live, plan, *rest):
    outs, picks, scratch = rest[:groups], rest[groups], rest[groups + 1 :]
    ids, weight, tokens, cots, slices, sems = scratch
    count, width = tokens.shape
    depth = width // groups
    small = fetch((ids_in, weight_in), (ids, weight), sems)
    large = []
    if depth % BLOCK == 0:
        cuts = [(slice(None), pl.ds(i * depth, depth)) for i in range(groups)]
    else:
        cuts = [(slice(None), slice(None))]
    for i, cut in enumerate(cuts):
        for source, target, sem in ((tokens_in, tokens, 2 + i), (cots_in, cots, 2 + groups + i)):
            large.append(pltpu.make_async_copy(source.at[cut], target.at[cut], sems.at[sem]))
            large[-1].start()
    for copy in small:
        copy.wait()
    lists = experts * ROWS
    slot = lax.broadcasted_iota(jnp.int32, (1, count), 1)
    line = lax.broadcasted_iota(jnp.int32, (lists, count), 0)
    alive = slot < live[...]
    odd = slot % 2 == 1
    listed = jnp.zeros((lists, count), F32)
    weights = jnp.zeros((lists, count), F32)
    for e in range(experts):
        match = ids[...] == e
        routed = (jnp.sum(jnp.where(match, 1.0, 0.0), axis=0, keepdims=True) > 0.0) & alive
        total = jnp.sum(jnp.where(match, weight[...], 0.0), axis=0, keepdims=True)
        second = odd & (plan[:, e : e + 1] == 1)
        in_first = jnp.where(routed & ~second, 1.0, 0.0)
        in_second = jnp.where(routed & second, 1.0, 0.0)
        is_first = (line >= e * ROWS) & (line < e * ROWS + CAP)
        is_second = (line >= e * ROWS + CAP) & (line < (e + 1) * ROWS)
        listed = jnp.where(is_first, in_first, jnp.where(is_second, in_second, listed))
        weights = jnp.where(is_first | is_second, total, weights)
    before = lax.broadcasted_iota(jnp.int32, (count, count), 0)
    here = lax.broadcasted_iota(jnp.int32, (count, count), 1)
    upto = jnp.where(before <= here, 1.0, 0.0).astype(BF16)
    place = mm(listed.astype(BF16), upto, NN)
    wanted = (line % CAP + 1).astype(F32)
    picked = jnp.where((listed > 0.0) & (place == wanted), 1.0, 0.0)
    column = jnp.sum(picked * weights, axis=1, keepdims=True)
    for e in range(experts):
        picks[e] = rows_of(picked, e * ROWS)
    picked = picked.astype(BF16)
    for s in range(groups):
        for copy in large[2 * s : 2 * s + 2]:
            copy.wait()
        cut = slice(s * depth, (s + 1) * depth)
        token_rows = mm(picked, tokens[:, cut], NN)
        cot_rows = mm(picked, cots[:, cut], NN) * column
        parts = []
        for e in range(experts):
            parts += [rows_of(token_rows, e * ROWS), rows_of(cot_rows, e * ROWS)]
        slices[s] = jnp.concatenate(parts, axis=0).astype(BF16)
    for k in range(groups):
        outs[k][...] = slices[lax.axis_index("dp") ^ k]


def weights_kernel(scale_gate, scale_up, scale_down, gate, up, down, gate_up, down_out, packed):
    depth, hid = gate.shape
    first = lax.axis_index("dp") * depth
    step = math.gcd(depth, BLOCK)
    for i in range(depth // step):
        block = (first + i * step) // BLOCK
        for h in range(hid // BLOCK):
            at = (slice(i * step, (i + 1) * step), slice(h * BLOCK, (h + 1) * BLOCK))
            to = (at[0], slice(hid + h * BLOCK, hid + (h + 1) * BLOCK))
            for out in (gate_up, packed):
                out[at] = (gate[at].astype(F32) * scale_gate[h, block]).astype(BF16)
                out[to] = (up[at].astype(F32) * scale_up[h, block]).astype(BF16)
    lane = lax.broadcasted_iota(jnp.int32, (1, depth), 1)
    start = first // BLOCK
    last = scale_down.shape[1] - 1
    for h in range(hid // BLOCK):
        spread = jnp.zeros((1, depth), F32) + scale_down[h, start]
        for j in range(1, depth // BLOCK + 2):
            block = jnp.minimum(start + j, last)
            spread = jnp.where(lane >= (start + j) * BLOCK - first, scale_down[h, block], spread)
        at = slice(h * BLOCK, (h + 1) * BLOCK)
        value = (down[at, :].astype(F32) * spread).astype(BF16)
        down_out[at, :] = value
        for i, (begin, end) in enumerate(pieces(depth, 2 * hid)):
            top = depth + i * hid + h * BLOCK
            packed[top : top + BLOCK, : end - begin] = value[:, begin:end]


def pieces(length, size):
    return [(i, min(i + size, length)) for i in range(0, length, size)]


def token_part(chunks):
    return jnp.concatenate([c[: c.shape[0] // 2, :] for c in chunks], axis=0)


def cot_part(chunks):
    return jnp.concatenate([c[c.shape[0] // 2 :, :] for c in chunks], axis=0)


def partial_kernel(groups, chips, *refs):
    chunks, (gate_up, down, packed), outs = refs[:chips], refs[chips : chips + 3], refs[chips + 3 :]
    tokens, cots = token_part(chunks), cot_part(chunks)
    outs[groups][...] = jnp.concatenate([tokens, cots], axis=0)
    hid, depth = down.shape
    dh = 0.0
    for i, (begin, end) in enumerate(pieces(depth, 2 * hid)):
        top = depth + i * hid
        dh = dh + mm(cots[:, begin:end], packed[top : top + hid, : end - begin], NT)
    products = (
        (mm(tokens, gate_up[...], NN), 0),
        (mm(cots, down[...], NT), 2 * hid),
        (mm(tokens, packed[:depth, :], NN), 3 * hid),
        (dh, 5 * hid),
    )
    for product, at in products:
        cut = slice(at, at + product.shape[1])
        for k in range(groups):
            rows = [rows_of(product, (c * groups + k) * ROWS) for c in range(chips)]
            outs[k][:, cut] = jnp.concatenate(rows, axis=0).astype(outs[k].dtype)


def act_kernel(groups, chips, *refs):
    parts, out, ordered = refs[:groups], refs[groups], refs[groups + 1]
    hid = out.shape[1] // 6
    for half in range(2):
        values = []
        for i in range(3):
            cut = slice((3 * half + i) * hid, (3 * half + i + 1) * hid)
            total = parts[0][:, cut]
            for part in parts[1:]:
                total = total + part[:, cut].astype(F32)
            values.append(total)
        a, b, dh = values
        sig = jax.nn.sigmoid(a)
        swish = a * sig
        results = (dh * b * sig * (1.0 + a * (1.0 - sig)), dh * swish, swish * b)
        for i, result in enumerate(results):
            cut = slice((3 * half + i) * hid, (3 * half + i + 1) * hid)
            for c in range(chips):
                ordered[(lax.axis_index("expert") // 2) ^ c, :, cut] = rows_of(result, c * ROWS)
    out[...] = jnp.concatenate([ordered[c] for c in range(chips)], axis=0).astype(BF16)


def dx_kernel(groups, chips, *refs):
    acts, (own, other, out) = refs[:groups], refs[groups:]
    depth, hid = own.shape[0], own.shape[1] // 2
    act = jnp.concatenate([a[...] for a in acts], axis=0)
    dx = mm(act[:, : 2 * hid], own[...], NT)
    dx = dx + mm(act[:, 3 * hid : 5 * hid], other[:depth, :], NT)
    count = chips * ROWS
    for k in range(groups):
        out[lax.axis_index("dp") ^ k] = dx[k * count : (k + 1) * count].astype(BF16)


def share_kernel(groups, *refs):
    half = refs[groups].shape[1]
    refs[groups][...] = jnp.concatenate([act[:, half:] for act in refs[:groups]], axis=0)


def place_kernel(groups, experts, chips, returned, picks, after, out, result, sems):
    depth = returned.shape[2]
    copies = []
    for s in range(groups):
        total = jnp.zeros((out.shape[0], depth), F32)
        for e in range(experts):
            rows = jnp.zeros((ROWS, depth), F32)
            for c in range(CHIPS):
                rows = rows + returned[s * chips + e * CHIPS + c].astype(F32)
            total = total + mm(picks[e].astype(BF16), rows.astype(BF16), TN)
        cut = slice(s * depth, (s + 1) * depth)
        result[:, cut] = total.astype(BF16)
        if depth % BLOCK == 0:
            copies.append(pltpu.make_async_copy(result.at[:, cut], out.at[:, cut], sems.at[s]))
            copies[-1].start()
    if not copies:
        copies.append(pltpu.make_async_copy(result, out, sems.at[0]))
        copies[-1].start()
    for copy in copies:
        copy.wait()


def grads_kernel(groups, chips, own, other, *refs):
    acts, act_other = refs[:groups], refs[groups]
    grad_gate, grad_up, grad_down, token, blocks = refs[groups + 1 :]
    hid, half, count = grad_gate.shape[1], own.shape[0] // 2, chips * ROWS
    tokens = jnp.concatenate([own[:half, :], other[:half, :]], axis=0)
    cots = jnp.concatenate([own[half:, :], other[half:, :]], axis=0)
    for k in range(groups):
        pair = acts[k][:, : 3 * hid], act_other[k * count : (k + 1) * count, :]
        for i, part in enumerate(pair):
            wide = part.astype(F32)
            for c in range(chips):
                blocks[i, k * chips + c] = rows_of(wide, c * ROWS)
    order = [
        blocks[i, k * chips + ((lax.axis_index("expert") // 2) ^ c)]
        for i in range(2)
        for c in range(chips)
        for k in range(groups)
    ]
    act = jnp.concatenate(order, axis=0).astype(BF16)
    grad_gate[...] = mm(tokens, act[:, :hid], TN).astype(BF16)
    grad_up[...] = mm(tokens, act[:, hid : 2 * hid], TN).astype(BF16)
    grad_down[...] = mm(act[:, 2 * hid :], cots, TN).astype(BF16)
    token[...] = jnp.zeros_like(token)


def chunk_of(parts, experts, slot):
    blocks = [p.reshape(experts, 2, ROWS, p.shape[1]) for p in parts]
    if experts == 1:
        blocks = [b[0] for b in blocks]
    else:
        blocks = [lax.dynamic_index_in_dim(b, slot, 0, keepdims=False) for b in blocks]
    return jnp.concatenate([b[0] for b in blocks] + [b[1] for b in blocks], axis=0)


def on_device(
    tokens,
    cotangent,
    route_weight,
    expert_ids,
    live_tokens,
    replica_plan,
    w_gate,
    w_up,
    w_down,
    scale_gate,
    scale_up,
    scale_down,
):
    members, groups = lax.axis_size("expert"), lax.axis_size("dp")
    experts, chips = members // HSH, members // 2
    count, width = tokens.shape
    depth, hid = w_gate.shape
    group, member = lax.axis_index("dp"), lax.axis_index("expert")
    rows = groups * chips * ROWS

    *sent, picks = call(
        functools.partial(route_kernel, groups, experts),
        [shape((2 * ROWS * experts, depth))] * groups + [shape((experts, ROWS, count), F32)],
        (),
        (live_tokens.reshape(1, 1), replica_plan),
        hbm=(expert_ids.T, route_weight.T, tokens, cotangent),
        scratch=[
            pltpu.VMEM(expert_ids.shape[::-1], jnp.int32),
            pltpu.VMEM(route_weight.shape[::-1], F32),
            pltpu.VMEM(tokens.shape, BF16),
            pltpu.VMEM(cotangent.shape, BF16),
            pltpu.VMEM((groups, 2 * ROWS * experts, depth), BF16),
            pltpu.SemaphoreType.DMA((2 + 2 * groups,)),
        ],
        flops=4 * count * experts * ROWS * width,
        limit=ROUTE_VMEM_BYTES,
        name="route",
    )
    parts = [sent[0]] + [swap(sent[k], "dp", k) for k in range(1, groups)]
    chunks = [chunk_of(parts, experts, member // HSH)]
    for c in range(1, chips):
        out = chunks[0] if experts == 1 else chunk_of(parts, experts, (member ^ (2 * c)) // HSH)
        chunks.append(swap(out, "expert", 2 * c))

    tall = depth + hid * len(pieces(depth, 2 * hid))
    gate_up, down, packed = call(
        weights_kernel,
        [shape((depth, 2 * hid)), shape((hid, depth)), shape((tall, 2 * hid))],
        (scale_gate.T, scale_up.T, scale_down),
        (w_gate, w_up, w_down),
        after=(parts[1],),
        flops=6 * depth * hid,
        name="weights",
    )
    other = swap(packed, "expert", 1)

    *partial, own_rows = call(
        functools.partial(partial_kernel, groups, chips),
        [shape((chips * ROWS, 6 * hid), F32 if k == 0 else BF16) for k in range(groups)]
        + [shape((2 * rows, depth))],
        (),
        (*chunks, gate_up, down, other),
        flops=12 * rows * depth * hid,
        name="partial",
    )
    other_rows = swap(own_rows, "expert", 1)
    summands = [partial[0]] + [swap(partial[k], "dp", k) for k in range(1, groups)]
    (act,) = call(
        functools.partial(act_kernel, groups, chips),
        [shape((chips * ROWS, 6 * hid))],
        (),
        summands,
        scratch=[pltpu.VMEM((chips, ROWS, 6 * hid), F32)],
        flops=40 * chips * ROWS * hid,
        name="activations",
    )
    acts = [act] + [swap(act, "dp", k) for k in range(1, groups)]
    (act_out,) = call(
        functools.partial(share_kernel, groups),
        [shape((rows, 3 * hid))],
        (),
        acts,
        name="share",
    )
    act_other = swap(act_out, "expert", 1)
    (dx,) = call(
        functools.partial(dx_kernel, groups, chips),
        [shape((groups, chips * ROWS, depth))],
        (),
        (*acts, gate_up, other),
        after=(act_out,),
        flops=8 * rows * depth * hid,
        name="dx",
    )
    dx = dx.reshape(groups * chips, ROWS, depth)
    same_core = [
        [g * members + 2 * c + core for g in range(groups) for c in range(chips)] for core in range(2)
    ]
    returned = lax.all_to_all(
        dx, ("dp", "expert"), split_axis=0, concat_axis=0, axis_index_groups=same_core, tiled=True
    )
    *grads, done = call(
        functools.partial(grads_kernel, groups, chips),
        [shape((depth, hid)), shape((depth, hid)), shape((hid, depth)), shape((8, BLOCK), F32)],
        (),
        (own_rows, other_rows, *acts, act_other),
        scratch=[pltpu.VMEM((2, groups * chips, ROWS, 3 * hid), F32)],
        flops=12 * rows * depth * hid,
        name="gradients",
    )
    (d_tokens,) = call(
        functools.partial(place_kernel, groups, experts, chips),
        [shape((count, width))],
        (),
        (returned, picks, done),
        far_out=True,
        scratch=[pltpu.VMEM((count, width), BF16), pltpu.SemaphoreType.DMA((groups,))],
        flops=2 * count * experts * ROWS * width,
        name="place",
    )
    return (d_tokens, *grads)


def solution(mesh):
    return jax.shard_map(
        on_device,
        mesh=mesh,
        in_specs=(
            P(("dp", "expert"), None),
            P(("dp", "expert"), None),
            P(("dp", "expert"), None),
            P(("dp", "expert"), None),
            P(("dp", "expert")),
            P(("dp", "expert"), None),
            P("dp", "expert"),
            P("dp", "expert"),
            P("expert", "dp"),
            P(None, "expert"),
            P(None, "expert"),
            P("expert", None),
        ),
        out_specs=(
            P(("dp", "expert"), None),
            P("dp", "expert"),
            P("dp", "expert"),
            P("expert", "dp"),
        ),
        check_vma=False,
    )
```

```python
import functools
import math

import jax
import jax.numpy as jnp
from jax import lax
from jax.experimental import pallas as pl
from jax.experimental.pallas import tpu as pltpu
from jax.sharding import PartitionSpec as P

HSH = 8
CAP = 4
ROWS = 2 * CAP
BLOCK = 128
CHIPS = HSH // 2
BF16 = jnp.bfloat16
F32 = jnp.float32
VMEM_BYTES = 40 * 1024 * 1024
MASKS_FLOPS = 1 << 29

NN = (((1,), (0,)), ((), ()))
NT = (((1,), (1,)), ((), ()))
TN = (((0,), (0,)), ((), ()))


def mm(a, b, dims):
    return lax.dot_general(a, b, dims, preferred_element_type=F32)


def call(kernel, outs, scalars, arrays, hbm=(), after=(), scratch=(), flops=0, name=None, far_out=False, limit=VMEM_BYTES):
    moved = sum(math.prod(x.shape) * x.dtype.itemsize for x in (*hbm, *arrays, *outs))
    count = len(scalars) + len(hbm)

    def body(*refs):
        kernel(*refs[:count], *refs[count + len(after) :])

    return pl.pallas_call(
        body,
        out_shape=outs,
        in_specs=[pl.BlockSpec(memory_space=pltpu.SMEM)] * len(scalars)
        + [pl.BlockSpec(memory_space=pltpu.HBM)] * len(hbm)
        + [pl.BlockSpec(memory_space=pltpu.VMEM)] * len(after)
        + [pl.BlockSpec(memory_space=pltpu.VMEM)] * len(arrays),
        out_specs=[pl.BlockSpec(memory_space=pltpu.HBM if far_out else pltpu.VMEM)] * len(outs),
        scratch_shapes=list(scratch),
        compiler_params=pltpu.CompilerParams(vmem_limit_bytes=limit),
        cost_estimate=pl.CostEstimate(flops=flops, bytes_accessed=moved, transcendentals=0),
        name=name,
    )(*scalars, *hbm, *after, *arrays)


def fetch(sources, targets, sems):
    copies = [pltpu.make_async_copy(s, t, sems.at[i]) for i, (s, t) in enumerate(zip(sources, targets))]
    for copy in copies:
        copy.start()
    return copies


def shape(dims, dtype=BF16):
    return jax.ShapeDtypeStruct(dims, dtype)


def swap(x, axis, k):
    return lax.ppermute(x, axis, [(i, i ^ k) for i in range(lax.axis_size(axis))])


def rows_of(value, first, count=ROWS):
    return value[first : first + count]


def masks_kernel(live, plan, masks):
    slot = lax.broadcasted_iota(jnp.int32, (1, masks.shape[1]), 1)
    masks[0:1, :] = jnp.where(slot < live[0], 1.0, 0.0)
    for e in range(plan.shape[1]):
        masks[e + 1 : e + 2, :] = jnp.where((slot % 2 == 1) & (plan[0, e] == 1), 1.0, 0.0)


def lists_kernel(experts, masks, ids, weight, picks, columns):
    count = ids.shape[1]
    lists = experts * ROWS
    line = lax.broadcasted_iota(jnp.int32, (lists, count), 0)
    alive = masks[0:1, :]
    listed = jnp.zeros((lists, count), F32)
    weights = jnp.zeros((lists, count), F32)
    for e in range(experts):
        match = ids[...] == e
        routed = jnp.sum(jnp.where(match, 1.0, 0.0), axis=0, keepdims=True)
        routed = jnp.where(routed > 0.0, alive, 0.0)
        total = jnp.sum(jnp.where(match, weight[...], 0.0), axis=0, keepdims=True)
        second = masks[e + 1 : e + 2, :]
        is_first = (line >= e * ROWS) & (line < e * ROWS + CAP)
        is_second = (line >= e * ROWS + CAP) & (line < (e + 1) * ROWS)
        listed = jnp.where(
            is_first, routed * (1.0 - second), jnp.where(is_second, routed * second, listed)
        )
        weights = jnp.where(is_first | is_second, total, weights)
    before = lax.broadcasted_iota(jnp.int32, (count, count), 0)
    here = lax.broadcasted_iota(jnp.int32, (count, count), 1)
    upto = jnp.where(before <= here, 1.0, 0.0).astype(BF16)
    place = mm(listed.astype(BF16), upto, NN)
    wanted = (line % CAP + 1).astype(F32)
    picked = jnp.where((listed > 0.0) & (place == wanted), 1.0, 0.0)
    column = jnp.sum(picked * weights, axis=1, keepdims=True)
    for e in range(experts):
        picks[e] = rows_of(picked, e * ROWS)
        columns[e] = jnp.broadcast_to(rows_of(column, e * ROWS), columns.shape[1:])


def route_kernel(groups, experts, picks, columns, tokens, cots, *rest):
    outs, slices = rest[:groups], rest[groups]
    depth = tokens.shape[1] // groups
    picked = jnp.concatenate([picks[e] for e in range(experts)], axis=0).astype(BF16)
    for s in range(groups):
        cut = slice(s * depth, (s + 1) * depth)
        token_rows = mm(picked, tokens[:, cut], NN)
        cot_rows = mm(picked, cots[:, cut], NN)
        parts = []
        for e in range(experts):
            weighted = rows_of(cot_rows, e * ROWS) * columns[e][:, :1]
            parts += [rows_of(token_rows, e * ROWS), weighted]
        slices[s] = jnp.concatenate(parts, axis=0).astype(BF16)
    for k in range(groups):
        outs[k][...] = slices[lax.axis_index("dp") ^ k]


def weights_kernel(scale_gate, scale_up, scale_down, gate, up, down, gate_up, down_out, packed):
    depth, hid = gate.shape
    first = lax.axis_index("dp") * depth
    step = math.gcd(depth, BLOCK)
    for i in range(depth // step):
        block = (first + i * step) // BLOCK
        for h in range(hid // BLOCK):
            at = (slice(i * step, (i + 1) * step), slice(h * BLOCK, (h + 1) * BLOCK))
            to = (at[0], slice(hid + h * BLOCK, hid + (h + 1) * BLOCK))
            for out in (gate_up, packed):
                out[at] = (gate[at].astype(F32) * scale_gate[h, block]).astype(BF16)
                out[to] = (up[at].astype(F32) * scale_up[h, block]).astype(BF16)
    lane = lax.broadcasted_iota(jnp.int32, (1, depth), 1)
    start = first // BLOCK
    last = scale_down.shape[1] - 1
    for h in range(hid // BLOCK):
        spread = jnp.zeros((1, depth), F32) + scale_down[h, start]
        for j in range(1, depth // BLOCK + 2):
            block = jnp.minimum(start + j, last)
            spread = jnp.where(lane >= (start + j) * BLOCK - first, scale_down[h, block], spread)
        at = slice(h * BLOCK, (h + 1) * BLOCK)
        value = (down[at, :].astype(F32) * spread).astype(BF16)
        down_out[at, :] = value
        for i, (begin, end) in enumerate(pieces(depth, 2 * hid)):
            top = depth + i * hid + h * BLOCK
            packed[top : top + BLOCK, : end - begin] = value[:, begin:end]


def pieces(length, size):
    return [(i, min(i + size, length)) for i in range(0, length, size)]


def token_part(chunks):
    return jnp.concatenate([c[: c.shape[0] // 2, :] for c in chunks], axis=0)


def cot_part(chunks):
    return jnp.concatenate([c[c.shape[0] // 2 :, :] for c in chunks], axis=0)


def partial_kernel(groups, chips, *refs):
    chunks, (gate_up, down, packed), outs = refs[:chips], refs[chips : chips + 3], refs[chips + 3 :]
    tokens, cots = token_part(chunks), cot_part(chunks)
    outs[groups][...] = jnp.concatenate([tokens, cots], axis=0)
    hid, depth = down.shape
    dh = 0.0
    for i, (begin, end) in enumerate(pieces(depth, 2 * hid)):
        top = depth + i * hid
        dh = dh + mm(cots[:, begin:end], packed[top : top + hid, : end - begin], NT)
    products = (
        (mm(tokens, gate_up[...], NN), 0),
        (mm(cots, down[...], NT), 2 * hid),
        (mm(tokens, packed[:depth, :], NN), 3 * hid),
        (dh, 5 * hid),
    )
    for product, at in products:
        cut = slice(at, at + product.shape[1])
        for k in range(groups):
            rows = [rows_of(product, (c * groups + k) * ROWS) for c in range(chips)]
            outs[k][:, cut] = jnp.concatenate(rows, axis=0).astype(outs[k].dtype)


def act_kernel(groups, chips, *refs):
    parts, out, ordered = refs[:groups], refs[groups], refs[groups + 1]
    hid = out.shape[1] // 6
    for half in range(2):
        values = []
        for i in range(3):
            cut = slice((3 * half + i) * hid, (3 * half + i + 1) * hid)
            total = parts[0][:, cut]
            for part in parts[1:]:
                total = total + part[:, cut].astype(F32)
            values.append(total)
        a, b, dh = values
        sig = jax.nn.sigmoid(a)
        swish = a * sig
        results = (dh * b * sig * (1.0 + a * (1.0 - sig)), dh * swish, swish * b)
        for i, result in enumerate(results):
            cut = slice((3 * half + i) * hid, (3 * half + i + 1) * hid)
            for c in range(chips):
                ordered[(lax.axis_index("expert") // 2) ^ c, :, cut] = rows_of(result, c * ROWS)
    out[...] = jnp.concatenate([ordered[c] for c in range(chips)], axis=0).astype(BF16)


def dx_kernel(groups, chips, *refs):
    acts, (own, other, out) = refs[:groups], refs[groups:]
    depth, hid = own.shape[0], own.shape[1] // 2
    act = jnp.concatenate([a[...] for a in acts], axis=0)
    dx = mm(act[:, : 2 * hid], own[...], NT)
    dx = dx + mm(act[:, 3 * hid : 5 * hid], other[:depth, :], NT)
    count = chips * ROWS
    for k in range(groups):
        out[lax.axis_index("dp") ^ k] = dx[k * count : (k + 1) * count].astype(BF16)


def share_kernel(groups, *refs):
    half = refs[groups].shape[1]
    refs[groups][...] = jnp.concatenate([act[:, half:] for act in refs[:groups]], axis=0)


def place_kernel(groups, experts, chips, returned, picks, after, out, result, sems):
    depth = returned.shape[2]
    copies = []
    for s in range(groups):
        total = jnp.zeros((out.shape[0], depth), F32)
        for e in range(experts):
            rows = jnp.zeros((ROWS, depth), F32)
            for c in range(CHIPS):
                rows = rows + returned[s * chips + e * CHIPS + c].astype(F32)
            total = total + mm(picks[e].astype(BF16), rows.astype(BF16), TN)
        cut = slice(s * depth, (s + 1) * depth)
        result[:, cut] = total.astype(BF16)
        if depth % BLOCK == 0:
            copies.append(pltpu.make_async_copy(result.at[:, cut], out.at[:, cut], sems.at[s]))
            copies[-1].start()
    if not copies:
        copies.append(pltpu.make_async_copy(result, out, sems.at[0]))
        copies[-1].start()
    for copy in copies:
        copy.wait()


def grads_kernel(groups, chips, own, other, *refs):
    acts, act_other = refs[:groups], refs[groups]
    grad_gate, grad_up, grad_down, token, blocks = refs[groups + 1 :]
    hid, half, count = grad_gate.shape[1], own.shape[0] // 2, chips * ROWS
    tokens = jnp.concatenate([own[:half, :], other[:half, :]], axis=0)
    cots = jnp.concatenate([own[half:, :], other[half:, :]], axis=0)
    for k in range(groups):
        pair = acts[k][:, : 3 * hid], act_other[k * count : (k + 1) * count, :]
        for i, part in enumerate(pair):
            wide = part.astype(F32)
            for c in range(chips):
                blocks[i, k * chips + c] = rows_of(wide, c * ROWS)
    order = [
        blocks[i, k * chips + ((lax.axis_index("expert") // 2) ^ c)]
        for i in range(2)
        for c in range(chips)
        for k in range(groups)
    ]
    act = jnp.concatenate(order, axis=0).astype(BF16)
    grad_gate[...] = mm(tokens, act[:, :hid], TN).astype(BF16)
    grad_up[...] = mm(tokens, act[:, hid : 2 * hid], TN).astype(BF16)
    grad_down[...] = mm(act[:, 2 * hid :], cots, TN).astype(BF16)
    token[...] = jnp.zeros_like(token)


def chunk_of(parts, experts, slot):
    blocks = [p.reshape(experts, 2, ROWS, p.shape[1]) for p in parts]
    if experts == 1:
        blocks = [b[0] for b in blocks]
    else:
        blocks = [lax.dynamic_index_in_dim(b, slot, 0, keepdims=False) for b in blocks]
    return jnp.concatenate([b[0] for b in blocks] + [b[1] for b in blocks], axis=0)


def on_device(
    tokens,
    cotangent,
    route_weight,
    expert_ids,
    live_tokens,
    replica_plan,
    w_gate,
    w_up,
    w_down,
    scale_gate,
    scale_up,
    scale_down,
):
    members, groups = lax.axis_size("expert"), lax.axis_size("dp")
    experts, chips = members // HSH, members // 2
    count, width = tokens.shape
    depth, hid = w_gate.shape
    group, member = lax.axis_index("dp"), lax.axis_index("expert")
    rows = groups * chips * ROWS

    (masks,) = call(
        masks_kernel,
        [shape((experts + 1, count), F32)],
        (live_tokens, replica_plan),
        (),
        flops=MASKS_FLOPS,
        name="masks",
    )
    picks, columns = call(
        functools.partial(lists_kernel, experts),
        [shape((experts, ROWS, count), F32), shape((experts, ROWS, BLOCK), F32)],
        (),
        (masks, expert_ids.T, route_weight.T),
        flops=2 * experts * ROWS * count * count,
        name="lists",
    )
    sent = call(
        functools.partial(route_kernel, groups, experts),
        [shape((2 * ROWS * experts, depth))] * groups,
        (),
        (picks, columns, tokens, cotangent),
        scratch=[pltpu.VMEM((groups, 2 * ROWS * experts, depth), BF16)],
        flops=4 * count * experts * ROWS * width,
        name="route",
    )
    parts = [sent[0]] + [swap(sent[k], "dp", k) for k in range(1, groups)]
    chunks = [chunk_of(parts, experts, member // HSH)]
    for c in range(1, chips):
        out = chunks[0] if experts == 1 else chunk_of(parts, experts, (member ^ (2 * c)) // HSH)
        chunks.append(swap(out, "expert", 2 * c))

    tall = depth + hid * len(pieces(depth, 2 * hid))
    gate_up, down, packed = call(
        weights_kernel,
        [shape((depth, 2 * hid)), shape((hid, depth)), shape((tall, 2 * hid))],
        (scale_gate.T, scale_up.T, scale_down),
        (w_gate, w_up, w_down),
        after=(parts[1],),
        flops=6 * depth * hid,
        name="weights",
    )
    other = swap(packed, "expert", 1)

    *partial, own_rows = call(
        functools.partial(partial_kernel, groups, chips),
        [shape((chips * ROWS, 6 * hid), F32 if k == 0 else BF16) for k in range(groups)]
        + [shape((2 * rows, depth))],
        (),
        (*chunks, gate_up, down, other),
        flops=12 * rows * depth * hid,
        name="partial",
    )
    other_rows = swap(own_rows, "expert", 1)
    summands = [partial[0]] + [swap(partial[k], "dp", k) for k in range(1, groups)]
    (act,) = call(
        functools.partial(act_kernel, groups, chips),
        [shape((chips * ROWS, 6 * hid))],
        (),
        summands,
        scratch=[pltpu.VMEM((chips, ROWS, 6 * hid), F32)],
        flops=40 * chips * ROWS * hid,
        name="activations",
    )
    acts = [act] + [swap(act, "dp", k) for k in range(1, groups)]
    (act_out,) = call(
        functools.partial(share_kernel, groups),
        [shape((rows, 3 * hid))],
        (),
        acts,
        name="share",
    )
    act_other = swap(act_out, "expert", 1)
    (dx,) = call(
        functools.partial(dx_kernel, groups, chips),
        [shape((groups, chips * ROWS, depth))],
        (),
        (*acts, gate_up, other),
        after=(act_out,),
        flops=8 * rows * depth * hid,
        name="dx",
    )
    dx = dx.reshape(groups * chips, ROWS, depth)
    same_core = [
        [g * members + 2 * c + core for g in range(groups) for c in range(chips)] for core in range(2)
    ]
    returned = lax.all_to_all(
        dx, ("dp", "expert"), split_axis=0, concat_axis=0, axis_index_groups=same_core, tiled=True
    )
    *grads, done = call(
        functools.partial(grads_kernel, groups, chips),
        [shape((depth, hid)), shape((depth, hid)), shape((hid, depth)), shape((8, BLOCK), F32)],
        (),
        (own_rows, other_rows, *acts, act_other),
        scratch=[pltpu.VMEM((2, groups * chips, ROWS, 3 * hid), F32)],
        flops=12 * rows * depth * hid,
        name="gradients",
    )
    (d_tokens,) = call(
        functools.partial(place_kernel, groups, experts, chips),
        [shape((count, width))],
        (),
        (returned, picks, done),
        far_out=True,
        scratch=[pltpu.VMEM((count, width), BF16), pltpu.SemaphoreType.DMA((groups,))],
        flops=2 * count * experts * ROWS * width,
        name="place",
    )
    return (d_tokens, *grads)


def solution(mesh):
    return jax.shard_map(
        on_device,
        mesh=mesh,
        in_specs=(
            P(("dp", "expert"), None),
            P(("dp", "expert"), None),
            P(("dp", "expert"), None),
            P(("dp", "expert"), None),
            P(("dp", "expert")),
            P(("dp", "expert"), None),
            P("dp", "expert"),
            P("dp", "expert"),
            P("expert", "dp"),
            P(None, "expert"),
            P(None, "expert"),
            P("expert", None),
        ),
        out_specs=(
            P(("dp", "expert"), None),
            P("dp", "expert"),
            P("dp", "expert"),
            P("expert", "dp"),
        ),
        check_vma=False,
    )
```

```python
import functools
import math

import jax
import jax.numpy as jnp
from jax import lax
from jax.experimental import pallas as pl
from jax.experimental.pallas import tpu as pltpu
from jax.sharding import PartitionSpec as P

HSH = 8
CAP = 4
ROWS = 2 * CAP
BLOCK = 128
CHIPS = HSH // 2
BF16 = jnp.bfloat16
F32 = jnp.float32
VMEM_BYTES = 40 * 1024 * 1024
MASKS_FLOPS = 1 << 29

NN = (((1,), (0,)), ((), ()))
NT = (((1,), (1,)), ((), ()))
TN = (((0,), (0,)), ((), ()))


def mm(a, b, dims):
    return lax.dot_general(a, b, dims, preferred_element_type=F32)


def call(kernel, outs, scalars, arrays, hbm=(), after=(), scratch=(), flops=0, name=None, far_out=False, limit=VMEM_BYTES):
    moved = sum(math.prod(x.shape) * x.dtype.itemsize for x in (*hbm, *arrays, *outs))
    count = len(scalars) + len(hbm)

    def body(*refs):
        kernel(*refs[:count], *refs[count + len(after) :])

    return pl.pallas_call(
        body,
        out_shape=outs,
        in_specs=[pl.BlockSpec(memory_space=pltpu.SMEM)] * len(scalars)
        + [pl.BlockSpec(memory_space=pltpu.HBM)] * len(hbm)
        + [pl.BlockSpec(memory_space=pltpu.VMEM)] * len(after)
        + [pl.BlockSpec(memory_space=pltpu.VMEM)] * len(arrays),
        out_specs=[pl.BlockSpec(memory_space=pltpu.HBM if far_out else pltpu.VMEM)] * len(outs),
        scratch_shapes=list(scratch),
        compiler_params=pltpu.CompilerParams(vmem_limit_bytes=limit),
        cost_estimate=pl.CostEstimate(flops=flops, bytes_accessed=moved, transcendentals=0),
        name=name,
    )(*scalars, *hbm, *after, *arrays)


def fetch(sources, targets, sems):
    copies = [pltpu.make_async_copy(s, t, sems.at[i]) for i, (s, t) in enumerate(zip(sources, targets))]
    for copy in copies:
        copy.start()
    return copies


def shape(dims, dtype=BF16):
    return jax.ShapeDtypeStruct(dims, dtype)


def swap(x, axis, k):
    return lax.ppermute(x, axis, [(i, i ^ k) for i in range(lax.axis_size(axis))])


def crossed(k):
    return k & ~3 | (k & 1) << 1 | (k >> 1) & 1


def partner(k):
    other = jnp.where(lax.axis_index("expert") % 2 == 1, crossed(k), k)
    return lax.axis_index("dp") ^ (k if crossed(k) == k else other)


def swap_slot(x, k):
    groups, members = lax.axis_size("dp"), lax.axis_size("expert")
    pairs = [
        (g * members + m, (g ^ (crossed(k) if m % 2 else k)) * members + m)
        for g in range(groups)
        for m in range(members)
    ]
    return lax.ppermute(x, ("dp", "expert"), pairs)


def rows_of(value, first, count=ROWS):
    return value[first : first + count]


def masks_kernel(live, plan, masks):
    slot = lax.broadcasted_iota(jnp.int32, (1, masks.shape[1]), 1)
    masks[0:1, :] = jnp.where(slot < live[0], 1.0, 0.0)
    for e in range(plan.shape[1]):
        masks[e + 1 : e + 2, :] = jnp.where((slot % 2 == 1) & (plan[0, e] == 1), 1.0, 0.0)


def lists_kernel(experts, masks, ids, weight, picks, columns):
    count = ids.shape[1]
    lists = experts * ROWS
    line = lax.broadcasted_iota(jnp.int32, (lists, count), 0)
    alive = masks[0:1, :]
    listed = jnp.zeros((lists, count), F32)
    weights = jnp.zeros((lists, count), F32)
    for e in range(experts):
        match = ids[...] == e
        routed = jnp.sum(jnp.where(match, 1.0, 0.0), axis=0, keepdims=True)
        routed = jnp.where(routed > 0.0, alive, 0.0)
        total = jnp.sum(jnp.where(match, weight[...], 0.0), axis=0, keepdims=True)
        second = masks[e + 1 : e + 2, :]
        is_first = (line >= e * ROWS) & (line < e * ROWS + CAP)
        is_second = (line >= e * ROWS + CAP) & (line < (e + 1) * ROWS)
        listed = jnp.where(
            is_first, routed * (1.0 - second), jnp.where(is_second, routed * second, listed)
        )
        weights = jnp.where(is_first | is_second, total, weights)
    before = lax.broadcasted_iota(jnp.int32, (count, count), 0)
    here = lax.broadcasted_iota(jnp.int32, (count, count), 1)
    upto = jnp.where(before <= here, 1.0, 0.0).astype(BF16)
    place = mm(listed.astype(BF16), upto, NN)
    wanted = (line % CAP + 1).astype(F32)
    picked = jnp.where((listed > 0.0) & (place == wanted), 1.0, 0.0)
    column = jnp.sum(picked * weights, axis=1, keepdims=True)
    for e in range(experts):
        picks[e] = rows_of(picked, e * ROWS)
        columns[e] = jnp.broadcast_to(rows_of(column, e * ROWS), columns.shape[1:])


def route_kernel(groups, experts, picks, columns, tokens, cots, *rest):
    outs, slices = rest[:groups], rest[groups]
    depth = tokens.shape[1] // groups
    picked = jnp.concatenate([picks[e] for e in range(experts)], axis=0).astype(BF16)
    for s in range(groups):
        cut = slice(s * depth, (s + 1) * depth)
        token_rows = mm(picked, tokens[:, cut], NN)
        cot_rows = mm(picked, cots[:, cut], NN)
        parts = []
        for e in range(experts):
            weighted = rows_of(cot_rows, e * ROWS) * columns[e][:, :1]
            parts += [rows_of(token_rows, e * ROWS), weighted]
        slices[s] = jnp.concatenate(parts, axis=0).astype(BF16)
    for k in range(groups):
        outs[k][...] = slices[partner(k)]


def weights_kernel(scale_gate, scale_up, scale_down, gate, up, down, gate_up, down_out, packed):
    depth, hid = gate.shape
    first = lax.axis_index("dp") * depth
    step = math.gcd(depth, BLOCK)
    for i in range(depth // step):
        block = (first + i * step) // BLOCK
        for h in range(hid // BLOCK):
            at = (slice(i * step, (i + 1) * step), slice(h * BLOCK, (h + 1) * BLOCK))
            to = (at[0], slice(hid + h * BLOCK, hid + (h + 1) * BLOCK))
            for out in (gate_up, packed):
                out[at] = (gate[at].astype(F32) * scale_gate[h, block]).astype(BF16)
                out[to] = (up[at].astype(F32) * scale_up[h, block]).astype(BF16)
    lane = lax.broadcasted_iota(jnp.int32, (1, depth), 1)
    start = first // BLOCK
    last = scale_down.shape[1] - 1
    for h in range(hid // BLOCK):
        spread = jnp.zeros((1, depth), F32) + scale_down[h, start]
        for j in range(1, depth // BLOCK + 2):
            block = jnp.minimum(start + j, last)
            spread = jnp.where(lane >= (start + j) * BLOCK - first, scale_down[h, block], spread)
        at = slice(h * BLOCK, (h + 1) * BLOCK)
        value = (down[at, :].astype(F32) * spread).astype(BF16)
        down_out[at, :] = value
        for i, (begin, end) in enumerate(pieces(depth, 2 * hid)):
            top = depth + i * hid + h * BLOCK
            packed[top : top + BLOCK, : end - begin] = value[:, begin:end]


def pieces(length, size):
    return [(i, min(i + size, length)) for i in range(0, length, size)]


def token_part(chunks):
    return jnp.concatenate([c[: c.shape[0] // 2, :] for c in chunks], axis=0)


def cot_part(chunks):
    return jnp.concatenate([c[c.shape[0] // 2 :, :] for c in chunks], axis=0)


def partial_kernel(groups, chips, *refs):
    chunks, (gate_up, down, packed), outs = refs[:chips], refs[chips : chips + 3], refs[chips + 3 :]
    tokens, cots = token_part(chunks), cot_part(chunks)
    outs[groups][...] = jnp.concatenate([tokens, cots], axis=0)
    hid, depth = down.shape
    dh = 0.0
    for i, (begin, end) in enumerate(pieces(depth, 2 * hid)):
        top = depth + i * hid
        dh = dh + mm(cots[:, begin:end], packed[top : top + hid, : end - begin], NT)
    products = (
        (mm(tokens, gate_up[...], NN), 0),
        (mm(cots, down[...], NT), 2 * hid),
        (mm(tokens, packed[:depth, :], NN), 3 * hid),
        (dh, 5 * hid),
    )
    for product, at in products:
        cut = slice(at, at + product.shape[1])
        for k in range(groups):
            rows = [rows_of(product, (c * groups + k) * ROWS) for c in range(chips)]
            outs[k][:, cut] = jnp.concatenate(rows, axis=0).astype(outs[k].dtype)


def act_kernel(groups, chips, *refs):
    parts, out, ordered = refs[:groups], refs[groups], refs[groups + 1]
    hid = out.shape[1] // 6
    for half in range(2):
        values = []
        for i in range(3):
            cut = slice((3 * half + i) * hid, (3 * half + i + 1) * hid)
            total = parts[0][:, cut]
            for part in parts[1:]:
                total = total + part[:, cut].astype(F32)
            values.append(total)
        a, b, dh = values
        sig = jax.nn.sigmoid(a)
        swish = a * sig
        results = (dh * b * sig * (1.0 + a * (1.0 - sig)), dh * swish, swish * b)
        for i, result in enumerate(results):
            cut = slice((3 * half + i) * hid, (3 * half + i + 1) * hid)
            for c in range(chips):
                ordered[(lax.axis_index("expert") // 2) ^ c, :, cut] = rows_of(result, c * ROWS)
    out[...] = jnp.concatenate([ordered[c] for c in range(chips)], axis=0).astype(BF16)


def dx_kernel(groups, chips, *refs):
    acts, (own, other, out) = refs[:groups], refs[groups:]
    depth, hid = own.shape[0], own.shape[1] // 2
    act = jnp.concatenate([a[...] for a in acts], axis=0)
    dx = mm(act[:, : 2 * hid], own[...], NT)
    dx = dx + mm(act[:, 3 * hid : 5 * hid], other[:depth, :], NT)
    count = chips * ROWS
    for k in range(groups):
        out[partner(k)] = dx[k * count : (k + 1) * count].astype(BF16)


def share_kernel(groups, *refs):
    half = refs[groups].shape[1]
    refs[groups][...] = jnp.concatenate([act[:, half:] for act in refs[:groups]], axis=0)


def place_kernel(groups, experts, chips, returned, picks, after, out, result, sems):
    depth = returned.shape[2]
    copies = []
    for s in range(groups):
        total = jnp.zeros((out.shape[0], depth), F32)
        for e in range(experts):
            rows = jnp.zeros((ROWS, depth), F32)
            for c in range(CHIPS):
                rows = rows + returned[s * chips + e * CHIPS + c].astype(F32)
            total = total + mm(picks[e].astype(BF16), rows.astype(BF16), TN)
        cut = slice(s * depth, (s + 1) * depth)
        result[:, cut] = total.astype(BF16)
        if depth % BLOCK == 0:
            copies.append(pltpu.make_async_copy(result.at[:, cut], out.at[:, cut], sems.at[s]))
            copies[-1].start()
    if not copies:
        copies.append(pltpu.make_async_copy(result, out, sems.at[0]))
        copies[-1].start()
    for copy in copies:
        copy.wait()


def grads_kernel(groups, chips, own, other, *refs):
    acts, act_other = refs[:groups], refs[groups]
    grad_gate, grad_up, grad_down, token, blocks = refs[groups + 1 :]
    hid, half, count = grad_gate.shape[1], own.shape[0] // 2, chips * ROWS
    tokens = jnp.concatenate([own[:half, :], other[:half, :]], axis=0)
    cots = jnp.concatenate([own[half:, :], other[half:, :]], axis=0)
    for k in range(groups):
        pair = acts[k][:, : 3 * hid], act_other[k * count : (k + 1) * count, :]
        for i, part in enumerate(pair):
            wide = part.astype(F32)
            for c in range(chips):
                blocks[i, k * chips + c] = rows_of(wide, c * ROWS)
    order = [
        blocks[i, k * chips + ((lax.axis_index("expert") // 2) ^ c)]
        for i in range(2)
        for c in range(chips)
        for k in range(groups)
    ]
    act = jnp.concatenate(order, axis=0).astype(BF16)
    grad_gate[...] = mm(tokens, act[:, :hid], TN).astype(BF16)
    grad_up[...] = mm(tokens, act[:, hid : 2 * hid], TN).astype(BF16)
    grad_down[...] = mm(act[:, 2 * hid :], cots, TN).astype(BF16)
    token[...] = jnp.zeros_like(token)


def chunk_of(parts, experts, slot):
    blocks = [p.reshape(experts, 2, ROWS, p.shape[1]) for p in parts]
    if experts == 1:
        blocks = [b[0] for b in blocks]
    else:
        blocks = [lax.dynamic_index_in_dim(b, slot, 0, keepdims=False) for b in blocks]
    return jnp.concatenate([b[0] for b in blocks] + [b[1] for b in blocks], axis=0)


def on_device(
    tokens,
    cotangent,
    route_weight,
    expert_ids,
    live_tokens,
    replica_plan,
    w_gate,
    w_up,
    w_down,
    scale_gate,
    scale_up,
    scale_down,
):
    members, groups = lax.axis_size("expert"), lax.axis_size("dp")
    experts, chips = members // HSH, members // 2
    count, width = tokens.shape
    depth, hid = w_gate.shape
    group, member = lax.axis_index("dp"), lax.axis_index("expert")
    rows = groups * chips * ROWS

    (masks,) = call(
        masks_kernel,
        [shape((experts + 1, count), F32)],
        (live_tokens, replica_plan),
        (),
        flops=MASKS_FLOPS,
        name="masks",
    )
    picks, columns = call(
        functools.partial(lists_kernel, experts),
        [shape((experts, ROWS, count), F32), shape((experts, ROWS, BLOCK), F32)],
        (),
        (masks, expert_ids.T, route_weight.T),
        flops=2 * experts * ROWS * count * count,
        name="lists",
    )
    sent = call(
        functools.partial(route_kernel, groups, experts),
        [shape((2 * ROWS * experts, depth))] * groups,
        (),
        (picks, columns, tokens, cotangent),
        scratch=[pltpu.VMEM((groups, 2 * ROWS * experts, depth), BF16)],
        flops=4 * count * experts * ROWS * width,
        name="route",
    )
    parts = [sent[0]] + [swap_slot(sent[k], k) for k in range(1, groups)]
    chunks = [chunk_of(parts, experts, member // HSH)]
    for c in range(1, chips):
        out = chunks[0] if experts == 1 else chunk_of(parts, experts, (member ^ (2 * c)) // HSH)
        chunks.append(swap(out, "expert", 2 * c))

    tall = depth + hid * len(pieces(depth, 2 * hid))
    gate_up, down, packed = call(
        weights_kernel,
        [shape((depth, 2 * hid)), shape((hid, depth)), shape((tall, 2 * hid))],
        (scale_gate.T, scale_up.T, scale_down),
        (w_gate, w_up, w_down),
        after=(parts[1],),
        flops=6 * depth * hid,
        name="weights",
    )
    other = swap(packed, "expert", 1)

    *partial, own_rows = call(
        functools.partial(partial_kernel, groups, chips),
        [shape((chips * ROWS, 6 * hid), F32 if k == 0 else BF16) for k in range(groups)]
        + [shape((2 * rows, depth))],
        (),
        (*chunks, gate_up, down, other),
        flops=12 * rows * depth * hid,
        name="partial",
    )
    other_rows = swap(own_rows, "expert", 1)
    summands = [partial[0]] + [swap_slot(partial[k], k) for k in range(1, groups)]
    (act,) = call(
        functools.partial(act_kernel, groups, chips),
        [shape((chips * ROWS, 6 * hid))],
        (),
        summands[:1] + summands[:0:-1],
        scratch=[pltpu.VMEM((chips, ROWS, 6 * hid), F32)],
        flops=40 * chips * ROWS * hid,
        name="activations",
    )
    acts = [act] + [swap_slot(act, k) for k in range(1, groups)]
    (act_out,) = call(
        functools.partial(share_kernel, groups),
        [shape((rows, 3 * hid))],
        (),
        acts,
        name="share",
    )
    act_other = swap(act_out, "expert", 1)
    (dx,) = call(
        functools.partial(dx_kernel, groups, chips),
        [shape((groups, chips * ROWS, depth))],
        (),
        (*acts, gate_up, other),
        after=(act_out,),
        flops=8 * rows * depth * hid,
        name="dx",
    )
    dx = dx.reshape(groups * chips, ROWS, depth)
    same_core = [
        [g * members + 2 * c + core for g in range(groups) for c in range(chips)] for core in range(2)
    ]
    returned = lax.all_to_all(
        dx, ("dp", "expert"), split_axis=0, concat_axis=0, axis_index_groups=same_core, tiled=True
    )
    *grads, done = call(
        functools.partial(grads_kernel, groups, chips),
        [shape((depth, hid)), shape((depth, hid)), shape((hid, depth)), shape((8, BLOCK), F32)],
        (),
        (own_rows, other_rows, *acts, act_other),
        scratch=[pltpu.VMEM((2, groups * chips, ROWS, 3 * hid), F32)],
        flops=12 * rows * depth * hid,
        name="gradients",
    )
    (d_tokens,) = call(
        functools.partial(place_kernel, groups, experts, chips),
        [shape((count, width))],
        (),
        (returned, picks, done),
        far_out=True,
        scratch=[pltpu.VMEM((count, width), BF16), pltpu.SemaphoreType.DMA((groups,))],
        flops=2 * count * experts * ROWS * width,
        name="place",
    )
    return (d_tokens, *grads)


def solution(mesh):
    return jax.shard_map(
        on_device,
        mesh=mesh,
        in_specs=(
            P(("dp", "expert"), None),
            P(("dp", "expert"), None),
            P(("dp", "expert"), None),
            P(("dp", "expert"), None),
            P(("dp", "expert")),
            P(("dp", "expert"), None),
            P("dp", "expert"),
            P("dp", "expert"),
            P("expert", "dp"),
            P(None, "expert"),
            P(None, "expert"),
            P("expert", None),
        ),
        out_specs=(
            P(("dp", "expert"), None),
            P("dp", "expert"),
            P("dp", "expert"),
            P("expert", "dp"),
        ),
        check_vma=False,
    )
```

```python
import functools
import math

import jax
import jax.numpy as jnp
from jax import lax
from jax.experimental import pallas as pl
from jax.experimental.pallas import tpu as pltpu
from jax.sharding import PartitionSpec as P

HSH = 8
CAP = 4
ROWS = 2 * CAP
BLOCK = 128
CHIPS = HSH // 2
BF16 = jnp.bfloat16
F32 = jnp.float32
VMEM_BYTES = 40 * 1024 * 1024
MASKS_FLOPS = 1 << 29

NN = (((1,), (0,)), ((), ()))
NT = (((1,), (1,)), ((), ()))
TN = (((0,), (0,)), ((), ()))


def mm(a, b, dims):
    return lax.dot_general(a, b, dims, preferred_element_type=F32)


def call(kernel, outs, scalars, arrays, hbm=(), after=(), scratch=(), flops=0, name=None, far_out=False, limit=VMEM_BYTES):
    moved = sum(math.prod(x.shape) * x.dtype.itemsize for x in (*hbm, *arrays, *outs))
    count = len(scalars) + len(hbm)

    def body(*refs):
        kernel(*refs[:count], *refs[count + len(after) :])

    return pl.pallas_call(
        body,
        out_shape=outs,
        in_specs=[pl.BlockSpec(memory_space=pltpu.SMEM)] * len(scalars)
        + [pl.BlockSpec(memory_space=pltpu.HBM)] * len(hbm)
        + [pl.BlockSpec(memory_space=pltpu.VMEM)] * len(after)
        + [pl.BlockSpec(memory_space=pltpu.VMEM)] * len(arrays),
        out_specs=[pl.BlockSpec(memory_space=pltpu.HBM if far_out else pltpu.VMEM)] * len(outs),
        scratch_shapes=list(scratch),
        compiler_params=pltpu.CompilerParams(vmem_limit_bytes=limit),
        cost_estimate=pl.CostEstimate(flops=flops, bytes_accessed=moved, transcendentals=0),
        name=name,
    )(*scalars, *hbm, *after, *arrays)


def fetch(sources, targets, sems):
    copies = [pltpu.make_async_copy(s, t, sems.at[i]) for i, (s, t) in enumerate(zip(sources, targets))]
    for copy in copies:
        copy.start()
    return copies


def shape(dims, dtype=BF16):
    return jax.ShapeDtypeStruct(dims, dtype)


def swap(x, axis, k):
    return lax.ppermute(x, axis, [(i, i ^ k) for i in range(lax.axis_size(axis))])


def crossed(k):
    return k & ~3 | (k & 1) << 1 | (k >> 1) & 1


def partner(k):
    other = jnp.where(lax.axis_index("expert") % 2 == 1, crossed(k), k)
    return lax.axis_index("dp") ^ (k if crossed(k) == k else other)


def neighbour(c, turn=0):
    other = jnp.where((lax.axis_index("expert") + turn) % 2 == 1, crossed(c), c)
    return (lax.axis_index("expert") // 2) ^ (c if crossed(c) == c else other)


def swap_chip(x, c):
    pairs = [(m, m ^ (2 * (crossed(c) if m % 2 else c))) for m in range(lax.axis_size("expert"))]
    return lax.ppermute(x, "expert", pairs)


def swap_slot(x, k):
    groups, members = lax.axis_size("dp"), lax.axis_size("expert")
    pairs = [
        (g * members + m, (g ^ (crossed(k) if m % 2 else k)) * members + m)
        for g in range(groups)
        for m in range(members)
    ]
    return lax.ppermute(x, ("dp", "expert"), pairs)


def rows_of(value, first, count=ROWS):
    return value[first : first + count]


def masks_kernel(live, plan, masks):
    slot = lax.broadcasted_iota(jnp.int32, (1, masks.shape[1]), 1)
    masks[0:1, :] = jnp.where(slot < live[0], 1.0, 0.0)
    for e in range(plan.shape[1]):
        masks[e + 1 : e + 2, :] = jnp.where((slot % 2 == 1) & (plan[0, e] == 1), 1.0, 0.0)


def lists_kernel(experts, masks, ids, weight, picks, columns):
    count = ids.shape[1]
    lists = experts * ROWS
    line = lax.broadcasted_iota(jnp.int32, (lists, count), 0)
    alive = masks[0:1, :]
    listed = jnp.zeros((lists, count), F32)
    weights = jnp.zeros((lists, count), F32)
    for e in range(experts):
        match = ids[...] == e
        routed = jnp.sum(jnp.where(match, 1.0, 0.0), axis=0, keepdims=True)
        routed = jnp.where(routed > 0.0, alive, 0.0)
        total = jnp.sum(jnp.where(match, weight[...], 0.0), axis=0, keepdims=True)
        second = masks[e + 1 : e + 2, :]
        is_first = (line >= e * ROWS) & (line < e * ROWS + CAP)
        is_second = (line >= e * ROWS + CAP) & (line < (e + 1) * ROWS)
        listed = jnp.where(
            is_first, routed * (1.0 - second), jnp.where(is_second, routed * second, listed)
        )
        weights = jnp.where(is_first | is_second, total, weights)
    before = lax.broadcasted_iota(jnp.int32, (count, count), 0)
    here = lax.broadcasted_iota(jnp.int32, (count, count), 1)
    upto = jnp.where(before <= here, 1.0, 0.0).astype(BF16)
    place = mm(listed.astype(BF16), upto, NN)
    wanted = (line % CAP + 1).astype(F32)
    picked = jnp.where((listed > 0.0) & (place == wanted), 1.0, 0.0)
    column = jnp.sum(picked * weights, axis=1, keepdims=True)
    for e in range(experts):
        picks[e] = rows_of(picked, e * ROWS)
        columns[e] = jnp.broadcast_to(rows_of(column, e * ROWS), columns.shape[1:])


def route_kernel(groups, experts, picks, columns, tokens, cots, *rest):
    outs, slices = rest[:groups], rest[groups]
    depth = tokens.shape[1] // groups
    picked = jnp.concatenate([picks[e] for e in range(experts)], axis=0).astype(BF16)
    for s in range(groups):
        cut = slice(s * depth, (s + 1) * depth)
        token_rows = mm(picked, tokens[:, cut], NN)
        cot_rows = mm(picked, cots[:, cut], NN)
        parts = []
        for e in range(experts):
            weighted = rows_of(cot_rows, e * ROWS) * columns[e][:, :1]
            parts += [rows_of(token_rows, e * ROWS), weighted]
        slices[s] = jnp.concatenate(parts, axis=0).astype(BF16)
    for k in range(groups):
        outs[k][...] = slices[partner(k)]


def weights_kernel(scale_gate, scale_up, scale_down, gate, up, down, gate_up, down_out, packed):
    depth, hid = gate.shape
    first = lax.axis_index("dp") * depth
    step = math.gcd(depth, BLOCK)
    for i in range(depth // step):
        block = (first + i * step) // BLOCK
        for h in range(hid // BLOCK):
            at = (slice(i * step, (i + 1) * step), slice(h * BLOCK, (h + 1) * BLOCK))
            to = (at[0], slice(hid + h * BLOCK, hid + (h + 1) * BLOCK))
            for out in (gate_up, packed):
                out[at] = (gate[at].astype(F32) * scale_gate[h, block]).astype(BF16)
                out[to] = (up[at].astype(F32) * scale_up[h, block]).astype(BF16)
    lane = lax.broadcasted_iota(jnp.int32, (1, depth), 1)
    start = first // BLOCK
    last = scale_down.shape[1] - 1
    for h in range(hid // BLOCK):
        spread = jnp.zeros((1, depth), F32) + scale_down[h, start]
        for j in range(1, depth // BLOCK + 2):
            block = jnp.minimum(start + j, last)
            spread = jnp.where(lane >= (start + j) * BLOCK - first, scale_down[h, block], spread)
        at = slice(h * BLOCK, (h + 1) * BLOCK)
        value = (down[at, :].astype(F32) * spread).astype(BF16)
        down_out[at, :] = value
        for i, (begin, end) in enumerate(pieces(depth, 2 * hid)):
            top = depth + i * hid + h * BLOCK
            packed[top : top + BLOCK, : end - begin] = value[:, begin:end]


def pieces(length, size):
    return [(i, min(i + size, length)) for i in range(0, length, size)]


def token_part(chunks):
    return jnp.concatenate([c[: c.shape[0] // 2, :] for c in chunks], axis=0)


def cot_part(chunks):
    return jnp.concatenate([c[c.shape[0] // 2 :, :] for c in chunks], axis=0)


def partial_kernel(groups, chips, *refs):
    chunks, (gate_up, down, packed), outs = refs[:chips], refs[chips : chips + 3], refs[chips + 3 :]
    tokens, cots = token_part(chunks), cot_part(chunks)
    outs[groups][...] = jnp.concatenate([tokens, cots], axis=0)
    hid, depth = down.shape
    dh = 0.0
    for i, (begin, end) in enumerate(pieces(depth, 2 * hid)):
        top = depth + i * hid
        dh = dh + mm(cots[:, begin:end], packed[top : top + hid, : end - begin], NT)
    products = (
        (mm(tokens, gate_up[...], NN), 0),
        (mm(cots, down[...], NT), 2 * hid),
        (mm(tokens, packed[:depth, :], NN), 3 * hid),
        (dh, 5 * hid),
    )
    for product, at in products:
        cut = slice(at, at + product.shape[1])
        for k in range(groups):
            rows = [rows_of(product, (c * groups + k) * ROWS) for c in range(chips)]
            outs[k][:, cut] = jnp.concatenate(rows, axis=0).astype(outs[k].dtype)


def act_kernel(groups, chips, *refs):
    parts, out, ordered = refs[:groups], refs[groups], refs[groups + 1]
    hid = out.shape[1] // 6
    for half in range(2):
        values = []
        for i in range(3):
            cut = slice((3 * half + i) * hid, (3 * half + i + 1) * hid)
            total = parts[0][:, cut]
            for part in parts[1:]:
                total = total + part[:, cut].astype(F32)
            values.append(total)
        a, b, dh = values
        sig = jax.nn.sigmoid(a)
        swish = a * sig
        results = (dh * b * sig * (1.0 + a * (1.0 - sig)), dh * swish, swish * b)
        for i, result in enumerate(results):
            cut = slice((3 * half + i) * hid, (3 * half + i + 1) * hid)
            for c in range(chips):
                ordered[neighbour(c), :, cut] = rows_of(result, c * ROWS)
    out[...] = jnp.concatenate([ordered[c] for c in range(chips)], axis=0).astype(BF16)


def dx_kernel(groups, chips, *refs):
    acts, (own, other, out) = refs[:groups], refs[groups:]
    depth, hid = own.shape[0], own.shape[1] // 2
    act = jnp.concatenate([a[...] for a in acts], axis=0)
    dx = mm(act[:, : 2 * hid], own[...], NT)
    dx = dx + mm(act[:, 3 * hid : 5 * hid], other[:depth, :], NT)
    count = chips * ROWS
    for k in range(groups):
        out[partner(k)] = dx[k * count : (k + 1) * count].astype(BF16)


def share_kernel(groups, *refs):
    half = refs[groups].shape[1]
    refs[groups][...] = jnp.concatenate([act[:, half:] for act in refs[:groups]], axis=0)


def place_kernel(groups, experts, chips, returned, picks, after, out, result, sems):
    depth = returned.shape[2]
    copies = []
    for s in range(groups):
        total = jnp.zeros((out.shape[0], depth), F32)
        for e in range(experts):
            rows = jnp.zeros((ROWS, depth), F32)
            for c in range(CHIPS):
                rows = rows + returned[s * chips + e * CHIPS + c].astype(F32)
            total = total + mm(picks[e].astype(BF16), rows.astype(BF16), TN)
        cut = slice(s * depth, (s + 1) * depth)
        result[:, cut] = total.astype(BF16)
        if depth % BLOCK == 0:
            copies.append(pltpu.make_async_copy(result.at[:, cut], out.at[:, cut], sems.at[s]))
            copies[-1].start()
    if not copies:
        copies.append(pltpu.make_async_copy(result, out, sems.at[0]))
        copies[-1].start()
    for copy in copies:
        copy.wait()


def grads_kernel(groups, chips, own, other, *refs):
    acts, act_other = refs[:groups], refs[groups]
    grad_gate, grad_up, grad_down, token, blocks = refs[groups + 1 :]
    hid, half, count = grad_gate.shape[1], own.shape[0] // 2, chips * ROWS
    tokens = jnp.concatenate([own[:half, :], other[:half, :]], axis=0)
    cots = jnp.concatenate([own[half:, :], other[half:, :]], axis=0)
    for k in range(groups):
        pair = acts[k][:, : 3 * hid], act_other[k * count : (k + 1) * count, :]
        for i, part in enumerate(pair):
            wide = part.astype(F32)
            for c in range(chips):
                blocks[i, k * chips + c] = rows_of(wide, c * ROWS)
    order = [
        blocks[i, k * chips + neighbour(c, i)]
        for i in range(2)
        for c in range(chips)
        for k in range(groups)
    ]
    act = jnp.concatenate(order, axis=0).astype(BF16)
    grad_gate[...] = mm(tokens, act[:, :hid], TN).astype(BF16)
    grad_up[...] = mm(tokens, act[:, hid : 2 * hid], TN).astype(BF16)
    grad_down[...] = mm(act[:, 2 * hid :], cots, TN).astype(BF16)
    token[...] = jnp.zeros_like(token)


def chunk_of(parts, experts, slot):
    blocks = [p.reshape(experts, 2, ROWS, p.shape[1]) for p in parts]
    if experts == 1:
        blocks = [b[0] for b in blocks]
    else:
        blocks = [lax.dynamic_index_in_dim(b, slot, 0, keepdims=False) for b in blocks]
    return jnp.concatenate([b[0] for b in blocks] + [b[1] for b in blocks], axis=0)


def on_device(
    tokens,
    cotangent,
    route_weight,
    expert_ids,
    live_tokens,
    replica_plan,
    w_gate,
    w_up,
    w_down,
    scale_gate,
    scale_up,
    scale_down,
):
    members, groups = lax.axis_size("expert"), lax.axis_size("dp")
    experts, chips = members // HSH, members // 2
    count, width = tokens.shape
    depth, hid = w_gate.shape
    group, member = lax.axis_index("dp"), lax.axis_index("expert")
    rows = groups * chips * ROWS

    (masks,) = call(
        masks_kernel,
        [shape((experts + 1, count), F32)],
        (live_tokens, replica_plan),
        (),
        flops=MASKS_FLOPS,
        name="masks",
    )
    picks, columns = call(
        functools.partial(lists_kernel, experts),
        [shape((experts, ROWS, count), F32), shape((experts, ROWS, BLOCK), F32)],
        (),
        (masks, expert_ids.T, route_weight.T),
        flops=2 * experts * ROWS * count * count,
        name="lists",
    )
    sent = call(
        functools.partial(route_kernel, groups, experts),
        [shape((2 * ROWS * experts, depth))] * groups,
        (),
        (picks, columns, tokens, cotangent),
        scratch=[pltpu.VMEM((groups, 2 * ROWS * experts, depth), BF16)],
        flops=4 * count * experts * ROWS * width,
        name="route",
    )
    parts = [sent[0]] + [swap_slot(sent[k], k) for k in range(1, groups)]
    chunks = [chunk_of(parts, experts, member // HSH)]
    for c in range(1, chips):
        out = chunks[0] if experts == 1 else chunk_of(parts, experts, (member ^ (2 * c)) // HSH)
        chunks.append(swap_chip(out, c))

    tall = depth + hid * len(pieces(depth, 2 * hid))
    gate_up, down, packed = call(
        weights_kernel,
        [shape((depth, 2 * hid)), shape((hid, depth)), shape((tall, 2 * hid))],
        (scale_gate.T, scale_up.T, scale_down),
        (w_gate, w_up, w_down),
        after=(parts[1],),
        flops=6 * depth * hid,
        name="weights",
    )
    other = swap(packed, "expert", 1)

    *partial, own_rows = call(
        functools.partial(partial_kernel, groups, chips),
        [shape((chips * ROWS, 6 * hid), F32 if k == 0 else BF16) for k in range(groups)]
        + [shape((2 * rows, depth))],
        (),
        (*chunks, gate_up, down, other),
        flops=12 * rows * depth * hid,
        name="partial",
    )
    other_rows = swap(own_rows, "expert", 1)
    summands = [partial[0]] + [swap_slot(partial[k], k) for k in range(1, groups)]
    (act,) = call(
        functools.partial(act_kernel, groups, chips),
        [shape((chips * ROWS, 6 * hid))],
        (),
        summands[:1] + summands[:0:-1],
        scratch=[pltpu.VMEM((chips, ROWS, 6 * hid), F32)],
        flops=40 * chips * ROWS * hid,
        name="activations",
    )
    acts = [act] + [swap_slot(act, k) for k in range(1, groups)]
    (act_out,) = call(
        functools.partial(share_kernel, groups),
        [shape((rows, 3 * hid))],
        (),
        acts,
        name="share",
    )
    act_other = swap(act_out, "expert", 1)
    (dx,) = call(
        functools.partial(dx_kernel, groups, chips),
        [shape((groups, chips * ROWS, depth))],
        (),
        (*acts, gate_up, other),
        after=(act_out,),
        flops=8 * rows * depth * hid,
        name="dx",
    )
    dx = dx.reshape(groups * chips, ROWS, depth)
    same_core = [
        [g * members + 2 * c + core for g in range(groups) for c in range(chips)] for core in range(2)
    ]
    returned = lax.all_to_all(
        dx, ("dp", "expert"), split_axis=0, concat_axis=0, axis_index_groups=same_core, tiled=True
    )
    *grads, done = call(
        functools.partial(grads_kernel, groups, chips),
        [shape((depth, hid)), shape((depth, hid)), shape((hid, depth)), shape((8, BLOCK), F32)],
        (),
        (own_rows, other_rows, *acts, act_other),
        scratch=[pltpu.VMEM((2, groups * chips, ROWS, 3 * hid), F32)],
        flops=12 * rows * depth * hid,
        name="gradients",
    )
    (d_tokens,) = call(
        functools.partial(place_kernel, groups, experts, chips),
        [shape((count, width))],
        (),
        (returned, picks, done),
        far_out=True,
        scratch=[pltpu.VMEM((count, width), BF16), pltpu.SemaphoreType.DMA((groups,))],
        flops=2 * count * experts * ROWS * width,
        name="place",
    )
    return (d_tokens, *grads)


def solution(mesh):
    return jax.shard_map(
        on_device,
        mesh=mesh,
        in_specs=(
            P(("dp", "expert"), None),
            P(("dp", "expert"), None),
            P(("dp", "expert"), None),
            P(("dp", "expert"), None),
            P(("dp", "expert")),
            P(("dp", "expert"), None),
            P("dp", "expert"),
            P("dp", "expert"),
            P("expert", "dp"),
            P(None, "expert"),
            P(None, "expert"),
            P("expert", None),
        ),
        out_specs=(
            P(("dp", "expert"), None),
            P("dp", "expert"),
            P("dp", "expert"),
            P("expert", "dp"),
        ),
        check_vma=False,
    )
```
